256 devices in a mesh: batch: 16 (over z, core), proto: 16 (over y, x).
Axes of the slice: x: 4, y: 4, z: 8, core: 2. Of those that a mesh axis runs over, the one named last changes fastest.
Arguments:
- student_features: bfloat16 [10, 2048, 256], P(None, 'batch'), may hold values from -8 to 8
- teacher_features: bfloat16 [2, 2048, 256], P(None, 'batch'), may hold values from -8 to 8
- student_prototypes: bfloat16 [256, 65536], P(None, 'proto'), may hold values from -0.5 to 0.5
- teacher_prototypes: bfloat16 [256, 65536], P(None, 'proto'), may hold values from -0.5 to 0.5
Outputs:
- mean_loss: float32 [], replicated
- grad_features: float32 [10, 2048, 256], P(None, ('batch', 'proto'))
- grad_prototypes: float32 [256, 65536], P('batch', 'proto')
The draws below stay inside these ranges and needn't reach their ends.
All inputs are finite; a program needn't handle non-finite values.
Results may differ from the reference program's by a relative error of at most 0.001.
The reference program's roundings to bfloat16 on the way (of `student_bf`, `proto_bf` and `grad_cos`) count: a program that leaves them out, or rounds other values in their place, can miss the bound.
Values sent between devices are 32-bit elements; how exact they have to be, the bound alone decides.
A program may use at most 192 MiB of HBM per device.

```python
import math
import jax
import jax.numpy as jnp
from jax import lax

D = 256
CLUSTER_NUMBER = 65536
CROPS = 10
WIDE_CROP_NUMBER = 2
SK_ITERS = 3
PICTURE_NUMBER = 2048
PAIRS = 18


def shared_parts(key):
    centers = jax.random.normal(jax.random.fold_in(key, 11), (8, D), jnp.float32)
    mixing = jax.random.normal(jax.random.fold_in(key, 13), (PICTURE_NUMBER, 8), jnp.float32)
    latent = jnp.dot(mixing, centers) / math.sqrt(8.0)
    labels = jax.random.randint(jax.random.fold_in(key, 17), (CLUSTER_NUMBER,), 0, 8)
    return (centers, latent, labels)


def crop_noise(key, shape):
    return jax.random.normal(key, shape, jnp.float32)


def draw_student_features(key, part):
    centers, latent, labels = shared_parts(key)
    noise = crop_noise(jax.random.fold_in(key, 21), (CROPS, PICTURE_NUMBER, D))
    values = 0.8 * latent[None] + 0.6 * noise
    return jnp.clip(values, -8.0, 8.0).astype(jnp.bfloat16)


def draw_teacher_features(key, part):
    centers, latent, labels = shared_parts(key)
    noise = crop_noise(jax.random.fold_in(key, 23), (WIDE_CROP_NUMBER, PICTURE_NUMBER, D))
    values = 0.9 * latent[None] + 0.45 * noise
    return jnp.clip(values, -8.0, 8.0).astype(jnp.bfloat16)


def proto_base(key):
    centers, latent, labels = shared_parts(key)
    noise = crop_noise(jax.random.fold_in(key, 31), (D, CLUSTER_NUMBER))
    return (0.7 * centers[labels].T + 0.7 * noise) / 16.0


def draw_student_prototypes(key, part):
    return jnp.clip(proto_base(key), -0.5, 0.5).astype(jnp.bfloat16)


def draw_teacher_prototypes(key, part):
    moved = proto_base(key) + 0.25 * jax.random.normal(jax.random.fold_in(key, 29), (D, CLUSTER_NUMBER), jnp.float32) / 16.0
    return jnp.clip(moved, -0.5, 0.5).astype(jnp.bfloat16)


def setup_inputs(seed: int = 0) -> dict:
    splits = jax.random.split(jax.random.key(seed), 5)
    return {
        "student_features": draw_student_features(jax.random.fold_in(splits[4], 71), 0),
        "teacher_features": draw_teacher_features(jax.random.fold_in(splits[4], 71), 0),
        "student_prototypes": draw_student_prototypes(jax.random.fold_in(splits[4], 71), 0),
        "teacher_prototypes": draw_teacher_prototypes(jax.random.fold_in(splits[4], 71), 0),
    }


STUDENT_TEMP = 0.1
TEACHER_TEMP = 0.07
NORM_EPS = 1e-06

def unit_rows(values):
    floats = values.astype(jnp.float32)
    inverse = lax.rsqrt(lax.optimization_barrier(jnp.sum(floats * floats, axis=-1, keepdims=True)) + NORM_EPS)
    return (floats * inverse, inverse)

def unit_columns(values):
    floats = values.astype(jnp.float32)
    inverse = lax.rsqrt(lax.optimization_barrier(jnp.sum(floats * floats, axis=0, keepdims=True)) + NORM_EPS)
    return (floats * inverse, inverse)

def equipartition_normalize(cluster_share, sample_number):
    for sweep_index in range(SK_ITERS):
        cluster_share = cluster_share / (CLUSTER_NUMBER * lax.optimization_barrier(jnp.sum(cluster_share, axis=0, keepdims=True)))
        cluster_share = cluster_share / (sample_number * lax.optimization_barrier(jnp.sum(cluster_share, axis=1, keepdims=True)))
    return sample_number * cluster_share

def reference(student_features, teacher_features, student_prototypes, teacher_prototypes):
    unit_student, student_scale = unit_rows(student_features)
    student_bf = unit_student.astype(jnp.bfloat16)
    unit_proto, proto_scale = unit_columns(student_prototypes)
    proto_bf = unit_proto.astype(jnp.bfloat16)
    unit_teacher, unused_scale = unit_rows(teacher_features)
    teacher_bf = unit_teacher.astype(jnp.bfloat16).reshape(WIDE_CROP_NUMBER * PICTURE_NUMBER, D)
    unit_tproto, unused_tscale = unit_columns(teacher_prototypes)
    teacher_proto_bf = unit_tproto.astype(jnp.bfloat16)
    mentor_logit_matrix = jnp.dot(teacher_bf, teacher_proto_bf, preferred_element_type=jnp.float32) / TEACHER_TEMP
    cluster_targets_matrix = equipartition_normalize(jnp.exp(mentor_logit_matrix), WIDE_CROP_NUMBER * PICTURE_NUMBER).reshape(WIDE_CROP_NUMBER, PICTURE_NUMBER, CLUSTER_NUMBER)
    first_global = cluster_targets_matrix[0]
    second_global = cluster_targets_matrix[1]
    summed = first_global + second_global
    factor = 1.0 / (PICTURE_NUMBER * PAIRS * STUDENT_TEMP)

    def crop_step(carried, inputs):
        weight_cot, curvature, loss_sum = carried
        crop_rows, crop_index = inputs
        logits = jnp.dot(crop_rows, proto_bf, preferred_element_type=jnp.float32) / STUDENT_TEMP
        log_norm = jnp.log(lax.optimization_barrier(jnp.sum(jnp.exp(logits), axis=1, keepdims=True)))
        targets = jnp.where(crop_index == 0, second_global, jnp.where(crop_index == 1, first_global, summed))
        pair_count = jnp.where(crop_index < 2, jnp.float32(1.0), jnp.float32(2.0))
        loss_sum = loss_sum + jnp.sum(targets * (log_norm - logits))
        grad_cos = ((pair_count * jnp.exp(logits - log_norm) - targets) * factor).astype(jnp.bfloat16)
        feature_cot = lax.dot_general(grad_cos, proto_bf, (((1,), (1,)), ((), ())), preferred_element_type=jnp.float32)
        weight_cot = weight_cot + lax.dot_general(crop_rows, grad_cos, (((0,), (0,)), ((), ())), preferred_element_type=jnp.float32)
        curvature = curvature + lax.optimization_barrier(jnp.sum(logits * STUDENT_TEMP * grad_cos.astype(jnp.float32), axis=0))
        return ((weight_cot, curvature, loss_sum), feature_cot)
    start = (jnp.zeros((D, CLUSTER_NUMBER), jnp.float32), jnp.zeros((CLUSTER_NUMBER,), jnp.float32), jnp.zeros((), jnp.float32))
    (weight_cot, curvature, loss_sum), feature_cot = lax.scan(crop_step, start, (student_bf, jnp.arange(CROPS, dtype=jnp.int32)))
    mean_loss = loss_sum / (PICTURE_NUMBER * PAIRS)
    grad_features = student_scale * (feature_cot - unit_student * lax.optimization_barrier(jnp.sum(unit_student * feature_cot, axis=-1, keepdims=True)))
    grad_prototypes = proto_scale * (weight_cot - unit_proto * curvature[None, :])
    return (mean_loss, grad_features, grad_prototypes)
```

```python
import functools
import math

import jax
import jax.numpy as jnp
import numpy as np
from jax import lax
from jax.experimental import pallas as pl
from jax.experimental.pallas import tpu as pltpu
from jax.sharding import PartitionSpec as P

WIDE = 2
SK_ITERS = 3
PAIRS = 18
CORES = 2
STUDENT_TEMP = 0.1
TEACHER_TEMP = 0.07
NORM_EPS = 1e-06
MESH = pl.DeviceIdType.MESH
F32 = jnp.float32
BF16 = jnp.bfloat16
WIDTH = 512


def inverse_norm(squares):
    return lax.rsqrt(squares + NORM_EPS)


def kernel(
    nb,
    np_,
    sf_ref,
    tf_ref,
    sp_ref,
    tp_ref,
    loss_ref,
    gf_ref,
    gp_ref,
    share,
    expo,
    mixed,
    sraw,
    sbf,
    st,
    mix,
    pbf,
    pscale,
    racc,
    scale,
    grad,
    cot,
    cot_in,
    wt,
    wt_core,
    wt_ring,
    rowb,
    mass_out,
    mass_in,
    col_own,
    col,
    row_out,
    row_in,
    exp_out,
    exp_in,
    loss_cols,
    loss_out,
    loss_in,
    ex_send,
    ex_recv,
    core_send,
    core_recv,
    ring_send,
    ring_recv,
):
    b = lax.axis_index("batch")
    p = lax.axis_index("proto")
    nz = nb // CORES
    z, core = lax.div(b, CORES), lax.rem(b, CORES)
    columns = share.shape[1]
    crops, images, depth = sraw.shape
    rows = crops * images
    part = columns // nb
    steps = columns // WIDTH
    own = images // np_
    images_all = images * nb
    teacher_rows = WIDE * images_all
    clusters = columns * np_
    factor = 1.0 / (images_all * PAIRS * STUDENT_TEMP)
    trows = WIDE * images

    def batch_peer(k):
        return lax.rem(b + k, nb)

    def proto_peer(k):
        return lax.rem(p + k, np_)

    def over_batch(make):
        def body(k, carry):
            make(batch_peer(k)).start()
            return carry

        lax.fori_loop(1, nb, body, 0)

    def over_proto(make):
        def body(k, carry):
            make(proto_peer(k)).start()
            return carry

        lax.fori_loop(1, np_, body, 0)

    def await_all(block, n, sem):
        view = block.at[pl.ds(0, n - 1)]
        pltpu.make_async_copy(view, view, sem).wait()

    tfl = tf_ref[...].astype(F32)
    tbf = (tfl * inverse_norm(jnp.sum(tfl * tfl, axis=1, keepdims=True))).astype(BF16)

    barrier = pltpu.get_barrier_semaphore()

    def greet_batch(k, carry):
        pl.semaphore_signal(barrier, inc=1, device_id={"batch": batch_peer(k)}, device_id_type=MESH)
        return carry

    def greet_proto(k, carry):
        pl.semaphore_signal(barrier, inc=1, device_id={"proto": proto_peer(k)}, device_id_type=MESH)
        return carry

    lax.fori_loop(1, nb, greet_batch, 0)
    lax.fori_loop(1, np_, greet_proto, 0)

    def teacher_step(j, carry):
        at = pl.ds(pl.multiple_of(j * part, part), part)
        values = tp_ref[:, at].astype(F32)
        unit = (values * inverse_norm(jnp.sum(values * values, axis=0, keepdims=True))).astype(BF16)
        e = jnp.exp2(
            jnp.dot(tbf, unit, preferred_element_type=F32) * (math.log2(math.e) / TEACHER_TEMP)
        )
        share[:, at] = e
        mass_out[0, pl.ds(j, 1)] = jnp.sum(e, axis=0, keepdims=True)[None]
        return carry

    lax.fori_loop(0, nb, teacher_step, 0)
    pl.semaphore_wait(barrier, nb - 1 + np_ - 1)

    def send_mass(it):
        over_batch(
            lambda q: pltpu.make_async_remote_copy(
                mass_out.at[it, q],
                mass_in.at[it, b],
                ex_send.at[it],
                ex_recv.at[it],
                device_id={"batch": q},
                device_id_type=MESH,
            )
        )

    def send_columns(it):
        await_all(mass_in.at[it], nb, ex_recv.at[it])
        mass_in[it, pl.ds(b, 1)] = mass_out[it, pl.ds(b, 1)]
        total = jnp.sum(mass_in[it], axis=0, keepdims=True)
        factors = 1.0 / (clusters * total)
        col_own[it] = factors
        over_batch(
            lambda q: pltpu.make_async_remote_copy(
                col_own.at[it, 0],
                col.at[it, b],
                ex_send.at[3 + it],
                ex_recv.at[3 + it],
                device_id={"batch": q},
                device_id_type=MESH,
            )
        )

    def send_rows(it):
        await_all(col.at[it], nb, ex_recv.at[3 + it])
        col[it, pl.ds(b, 1)] = col_own[it]

        def body(j, acc):
            at = pl.ds(pl.multiple_of(j * part, part), part)
            weighted = share[:, at] * col[it, j]
            if it == SK_ITERS - 1:
                share[:, at] = weighted
            for lane in range(0, part, 128):
                acc = acc + weighted[:, lane : lane + 128]
            return acc

        acc = lax.fori_loop(0, nb, body, jnp.zeros((trows, 128), F32))
        row_out[it] = jnp.sum(acc.T, axis=0, keepdims=True)
        over_proto(
            lambda q: pltpu.make_async_remote_copy(
                row_out.at[it],
                row_in.at[it, p],
                ex_send.at[6 + it],
                ex_recv.at[6 + it],
                device_id={"proto": q},
                device_id_type=MESH,
            )
        )

    def row_factors(it):
        await_all(row_in.at[it], np_, ex_recv.at[6 + it])
        row_in[it, pl.ds(p, 1)] = row_out[it][None]
        return 1.0 / jnp.sum(row_in[it], axis=0)

    def mass_of_rows(it, inverse):
        rowb[...] = jnp.broadcast_to(inverse * (1.0 / teacher_rows), (128, trows)).T

        def body(j, carry):
            for lane in range(0, part, 128):
                at = pl.ds(pl.multiple_of(j * part + lane, 128), 128)
                mass_out[it, j, :, lane : lane + 128] = jnp.sum(
                    share[:, at] * rowb[...], axis=0, keepdims=True
                )
            return carry

        lax.fori_loop(0, nb, body, 0)

    def student_rows():
        def body(c, carry):
            first, second = carry
            at = pl.ds(pl.multiple_of(c * images, images), images)
            values = sf_ref[at, :].astype(F32)
            sraw[c] = values
            unit = (values * inverse_norm(jnp.sum(values * values, axis=1, keepdims=True))).astype(BF16)
            sbf[at, :] = unit
            wide = unit.astype(F32)
            st[:, at] = wide.T.astype(BF16)
            first = first + jnp.where(c == 0, 0.0, 1.0) * wide
            second = second + jnp.where(c == 1, 0.0, 1.0) * wide
            return first, second

        zero = jnp.zeros((images, depth), F32)
        sums = lax.fori_loop(0, crops, body, (zero, zero))
        for i, values in enumerate(sums):
            high = values.astype(BF16)
            mix[i * images : (i + 1) * images, :] = high
            mix[trows + i * images : trows + (i + 1) * images, :] = (values - high.astype(F32)).astype(BF16)
        racc[...] = jnp.zeros_like(racc)

    def student_prototypes():
        def body(j, carry):
            at = pl.ds(pl.multiple_of(j * part, part), part)
            values = sp_ref[:, at].astype(F32)
            inverse = inverse_norm(jnp.sum(values * values, axis=0, keepdims=True))
            pscale[:, at] = inverse
            pbf[:, at] = (values * inverse).astype(BF16)
            return carry

        lax.fori_loop(0, nb, body, 0)

    def student_steps(low, high):
        def body(j, carry):
            at = pl.ds(pl.multiple_of(j * WIDTH, WIDTH), WIDTH)
            block = pbf[:, at]
            e = jnp.exp2(
                jnp.dot(sbf[...], block, preferred_element_type=F32) * (math.log2(math.e) / STUDENT_TEMP)
            )
            expo[:, at] = e
            acc = racc[...]
            for lane in range(0, WIDTH, 128):
                acc = acc + e[:, lane : lane + 128]
            racc[...] = acc
            both = jnp.dot(mix[...], block, preferred_element_type=F32)
            mixed[:, at] = (both[:trows] + both[trows:]) * (1.0 / STUDENT_TEMP)
            return carry

        lax.fori_loop(low, high, body, 0)

    def send_exponentials():
        for c in range(crops):
            exp_out[c] = jnp.sum(racc[c * images : (c + 1) * images, :].T, axis=0, keepdims=True)
        over_proto(
            lambda q: pltpu.make_async_remote_copy(
                exp_out,
                exp_in.at[p],
                ex_send.at[9],
                ex_recv.at[9],
                device_id={"proto": q},
                device_id_type=MESH,
            )
        )

    def student_scales():
        await_all(exp_in, np_, ex_recv.at[9])
        exp_in[pl.ds(p, 1)] = exp_out[...][None]
        for c in range(crops):
            total = jnp.sum(exp_in[:, c], axis=0)
            pairs = 1.0 if c < 2 else 2.0
            scale[c * images : (c + 1) * images, :] = jnp.broadcast_to(
                (pairs * factor) / total, (128, images)
            ).T

    cut = [0, steps // 4, steps // 2, 3 * steps // 4, steps]
    send_mass(0)
    student_rows()
    send_columns(0)
    student_prototypes()
    send_rows(0)
    student_steps(cut[0], cut[1])
    mass_of_rows(1, row_factors(0))
    send_mass(1)
    student_steps(cut[1], cut[2])
    send_columns(1)
    student_steps(cut[2], cut[3])
    send_rows(1)
    student_steps(cut[3], cut[4])
    mass_of_rows(2, row_factors(1))
    send_mass(2)
    send_exponentials()
    send_columns(2)
    loss_cols[...] = jnp.zeros_like(loss_cols)
    cot[...] = jnp.zeros_like(cot)
    student_scales()
    send_rows(2)
    last = row_factors(2)
    rowb[...] = jnp.broadcast_to(last * factor, (128, trows)).T

    def core_copy(t):
        return pltpu.make_async_remote_copy(
            wt.at[t, :, 1 - core],
            wt_core.at[t],
            core_send.at[t],
            core_recv.at[t],
            device_id={"batch": z * CORES + 1 - core},
            device_id_type=MESH,
        )

    def ring_copy(t, s):
        way = 1 - 2 * lax.rem(t, 2)
        segment = lax.rem(z - way * (1 + s) + 2 * nz, nz)
        to = lax.rem(z + way + nz, nz)
        return pltpu.make_async_remote_copy(
            wt.at[t, segment, core],
            wt_ring.at[t, s],
            ring_send.at[t, s],
            ring_recv.at[t, s],
            device_id={"batch": to * CORES + core},
            device_id_type=MESH,
        )

    def serve(t, phase):
        @pl.when(phase == 1)
        def _():
            core_copy(t).wait_recv()
            for segment in range(nz):
                wt[t, segment, pl.ds(core, 1)] += wt_core[t, pl.ds(segment, 1)]
            ring_copy(t, 0).start()

        @pl.when(jnp.logical_and(phase >= 2, phase <= nz))
        def _():
            s = phase - 2
            way = 1 - 2 * lax.rem(t, 2)
            segment = lax.rem(z - way * (2 + s) + 2 * nz, nz)
            ring_copy(t, s).wait_recv()
            wt[t, segment, core] += wt_ring[t, s]

            @pl.when(s < nz - 2)
            def _():
                ring_copy(t, s + 1).start()

            @pl.when(s == nz - 2)
            def _():
                at = pl.ds(pl.multiple_of(t * WIDTH, WIDTH), WIDTH)
                gp_ref[:, at] = pscale[:, at] * wt[t, z, core]

    def serve_all(k):
        def body(t, carry):
            serve(t, k - t)
            return carry

        lax.fori_loop(0, jnp.minimum(k, steps), body, 0)

    def gradient_step(j, carry):
        at = pl.ds(pl.multiple_of(j * WIDTH, WIDTH), WIDTH)
        loss_acc = loss_cols[...]
        row0 = jnp.concatenate([rowb[:images, :]] * (WIDTH // 128), axis=1)
        row1 = jnp.concatenate([rowb[images:, :]] * (WIDTH // 128), axis=1)
        first = share[:images, at] * row0
        second = share[images:, at] * row1
        loss_acc = loss_acc + jnp.sum(first * mixed[:images, at], axis=0, keepdims=True)
        loss_acc = loss_acc + jnp.sum(second * mixed[images:, at], axis=0, keepdims=True)
        loss_cols[...] = loss_acc
        both = first + second
        for c in range(crops):
            own_rows = slice(c * images, (c + 1) * images)
            target = second if c == 0 else first if c == 1 else both
            scales = jnp.concatenate([scale[own_rows, :]] * (WIDTH // 128), axis=1)
            grad[own_rows, :] = (expo[own_rows, at] * scales - target).astype(BF16)
        block = pbf[:, at]
        g = grad[...]
        product = jnp.dot(st[...], g, preferred_element_type=F32)
        inverse = pscale[:, at]
        unit = sp_ref[:, at].astype(F32) * inverse
        curvature = jnp.sum(block.astype(F32) * product, axis=0, keepdims=True)
        wt[j] = (product - unit * curvature).reshape(wt.shape[1:])
        core_copy(j).start()
        cot[...] += lax.dot_general(g, block, (((1,), (1,)), ((), ())), preferred_element_type=F32).reshape(
            cot.shape
        )
        serve_all(j)
        return carry

    lax.fori_loop(0, steps, gradient_step, 0)

    over_proto(
        lambda q: pltpu.make_async_remote_copy(
            cot.at[:, pl.ds(pl.multiple_of(q * own, own), own)],
            cot_in.at[p],
            ex_send.at[12],
            ex_recv.at[12],
            device_id={"proto": q},
            device_id_type=MESH,
        )
    )

    portion = row_out[SK_ITERS - 1] * last
    logs = [jnp.log(jnp.sum(exp_in[:, c], axis=0)) for c in range(crops)]
    shared = functools.reduce(lambda x, y: x + y, logs[2:])
    lossv = portion[:, :images] * (logs[1] + shared) + portion[:, images:] * (logs[0] + shared)
    for lane in range(0, WIDTH, 128):
        lossv = lossv - loss_cols[:, lane : lane + 128] * (1.0 / factor)
    loss_out[0] = lossv
    over_proto(
        lambda q: pltpu.make_async_remote_copy(
            loss_out.at[0],
            loss_in.at[0, p],
            ex_send.at[10],
            ex_recv.at[10],
            device_id={"proto": q},
            device_id_type=MESH,
        )
    )

    def tail(k, carry):
        serve_all(k)
        return carry

    lax.fori_loop(steps, steps + 2, tail, 0)
    await_all(loss_in.at[0], np_, ex_recv.at[10])
    loss_in[0, pl.ds(p, 1)] = loss_out[0][None]
    loss_out[1] = jnp.sum(loss_in[0, :np_], axis=0)
    over_batch(
        lambda q: pltpu.make_async_remote_copy(
            loss_out.at[1],
            loss_in.at[1, b],
            ex_send.at[11],
            ex_recv.at[11],
            device_id={"batch": q},
            device_id_type=MESH,
        )
    )
    lax.fori_loop(steps + 2, steps + nz + 1, tail, 0)

    await_all(loss_in.at[1], nb, ex_recv.at[11])
    loss_in[1, pl.ds(b, 1)] = loss_out[1][None]
    total = jnp.sum(loss_in[1, :nb], axis=0)
    loss_ref[...] = jnp.sum(total, axis=1, keepdims=True) * (1.0 / (images_all * PAIRS))

    await_all(cot_in, np_, ex_recv.at[12])
    mine = pl.ds(pl.multiple_of(p * own, own), own)
    cot_in[pl.ds(p, 1)] = cot[:, mine][None]
    total = jnp.sum(cot_in[...], axis=0)
    values = sraw[:, mine]
    inverse = inverse_norm(jnp.sum(values * values, axis=2, keepdims=True))
    unit = values * inverse
    gf_ref[...] = inverse * (total - unit * jnp.sum(unit * total, axis=2, keepdims=True))

    for it in range(SK_ITERS):
        await_all(mass_out.at[it], nb, ex_send.at[it])
        await_all(col.at[it], nb, ex_send.at[3 + it])
        await_all(row_in.at[it], np_, ex_send.at[6 + it])
    await_all(exp_in, np_, ex_send.at[9])
    await_all(loss_in.at[0], np_, ex_send.at[10])
    await_all(loss_in.at[1], nb, ex_send.at[11])
    await_all(cot_in, np_, ex_send.at[12])

    def sent(t, carry):
        core_copy(t).wait_send()

        def one(s, c):
            ring_copy(t, s).wait_send()
            return c

        lax.fori_loop(0, nz - 1, one, 0)
        return carry

    lax.fori_loop(0, steps, sent, 0)


def on_device(student_features, teacher_features, student_prototypes, teacher_prototypes):
    crops, images, depth = student_features.shape
    columns = student_prototypes.shape[1]
    nb, np_ = lax.axis_size("batch"), lax.axis_size("proto")
    nz = nb // CORES
    rows, trows = crops * images, WIDE * images
    steps, part, deep = columns // WIDTH, columns // nb, depth // nb
    vmem = pltpu.VMEM
    dma = pltpu.SemaphoreType.DMA
    loss, grad_features, grad_prototypes = pl.pallas_call(
        functools.partial(kernel, nb, np_),
        out_shape=(
            jax.ShapeDtypeStruct((1, 1), F32),
            jax.ShapeDtypeStruct((crops, images // np_, depth), F32),
            jax.ShapeDtypeStruct((deep, columns), F32),
        ),
        in_specs=[pl.BlockSpec(memory_space=vmem)] * 4,
        out_specs=[pl.BlockSpec(memory_space=vmem)] * 3,
        scratch_shapes=[
            vmem((trows, columns), F32),
            vmem((rows, columns), F32),
            vmem((trows, columns), F32),
            vmem((crops, images, depth), F32),
            vmem((rows, depth), BF16),
            vmem((depth, rows), BF16),
            vmem((2 * trows, depth), BF16),
            vmem((depth, columns), BF16),
            vmem((1, columns), F32),
            vmem((rows, 128), F32),
            vmem((rows, 128), F32),
            vmem((rows, WIDTH), BF16),
            vmem((crops, images, depth), F32),
            vmem((np_, crops, images // np_, depth), F32),
            vmem((steps, nz, CORES, deep, WIDTH), F32),
            vmem((steps, nz, deep, WIDTH), F32),
            vmem((steps, nz - 1, deep, WIDTH), F32),
            vmem((trows, 128), F32),
            vmem((SK_ITERS, nb, 1, part), F32),
            vmem((SK_ITERS, nb, 1, part), F32),
            vmem((SK_ITERS, 1, 1, part), F32),
            vmem((SK_ITERS, nb, 1, part), F32),
            vmem((SK_ITERS, 1, trows), F32),
            vmem((SK_ITERS, np_, 1, trows), F32),
            vmem((crops, 1, images), F32),
            vmem((np_, crops, 1, images), F32),
            vmem((1, WIDTH), F32),
            vmem((2, 1, 128), F32),
            vmem((2, max(nb, np_), 1, 128), F32),
            dma((13,)),
            dma((13,)),
            dma((steps,)),
            dma((steps,)),
            dma((steps, nz - 1)),
            dma((steps, nz - 1)),
        ],
        compiler_params=pltpu.CompilerParams(
            collective_id=0, has_side_effects=True, vmem_limit_bytes=62 * 1024 * 1024
        ),
    )(
        student_features.reshape(rows, depth),
        teacher_features.reshape(trows, depth),
        student_prototypes,
        teacher_prototypes,
    )
    return loss[0, 0], grad_features, grad_prototypes


def solution(mesh):
    return jax.shard_map(
        on_device,
        mesh=mesh,
        in_specs=(P(None, "batch", None), P(None, "batch", None), P(None, "proto"), P(None, "proto")),
        out_specs=(P(), P(None, ("batch", "proto"), None), P("batch", "proto")),
        check_vma=False,
    )
```

```python
import functools
import math

import jax
import jax.numpy as jnp
from jax import lax
from jax.experimental import pallas as pl
from jax.experimental.pallas import tpu as pltpu
from jax.sharding import PartitionSpec as P

WIDE = 2
SK_ITERS = 3
PAIRS = 18
CORES = 2
STUDENT_TEMP = 0.1
TEACHER_TEMP = 0.07
NORM_EPS = 1e-06
MESH = pl.DeviceIdType.MESH
F32 = jnp.float32
BF16 = jnp.bfloat16
WIDTH = 512
PART = 256
LAG = 4
GROUPS = 2


def inverse_norm(squares):
    return lax.rsqrt(squares + NORM_EPS)


def kernel(
    nb,
    np_,
    sf_hbm,
    tf_hbm,
    sp_hbm,
    tp_hbm,
    loss_ref,
    gf_ref,
    gp_ref,
    sf_ref,
    tf_ref,
    sp_ref,
    pbf,
    tbf,
    tsend,
    trecv,
    share,
    expo,
    mixed,
    sraw,
    sbf,
    st,
    mix,
    pscale,
    racc,
    scale,
    grad,
    cot,
    cot_in,
    wt,
    wt_core,
    wt_ring,
    rowb,
    mass_out,
    mass_in,
    col,
    row_out,
    row_in,
    row_inv,
    exp_out,
    exp_in,
    loss_cols,
    loss_out,
    loss_plane,
    loss_z,
    load_sem,
    ex_send,
    ex_recv,
    cot_send,
    cot_recv,
    core_send,
    core_recv,
    ring_send,
    ring_recv,
):
    b = lax.axis_index("batch")
    p = lax.axis_index("proto")
    nz = nb // CORES
    z, core = lax.div(b, CORES), lax.rem(b, CORES)
    other = 1 - core
    half = share.shape[2]
    lanes = half // 128
    columns = CORES * half
    crops, images, depth = sraw.shape
    steps = columns // WIDTH
    own = images // np_
    images_all = images * nb
    teacher_rows = WIDE * images_all
    clusters = columns * np_
    factor = 1.0 / (images_all * PAIRS * STUDENT_TEMP)
    trows = WIDE * images
    plane = CORES * np_
    here = core * np_ + p
    hops = (nz // 2, nz - 1 - nz // 2)

    z_peers = [{"batch": lax.rem(z + k, nz) * CORES + core} for k in range(1, nz)]
    proto_peers = [lax.rem(p + k, np_) for k in range(1, np_)]
    plane_peers = [{"proto": q} for q in proto_peers]
    plane_peers += [{"batch": z * CORES + other, "proto": q} for q in proto_peers]
    plane_peers += [{"batch": z * CORES + other}]

    def send(peers, source, target, sends, receives):
        for peer in peers:
            pltpu.make_async_remote_copy(
                source, target, sends, receives, device_id=peer, device_id_type=MESH
            ).start()

    def await_all(block, n, sem):
        view = block.at[pl.ds(0, n - 1)]
        pltpu.make_async_copy(view, view, sem).wait()

    def half_of(ref, which):
        return ref.at[:, pl.ds(pl.multiple_of(which * half, half), half)]

    loads = [
        pltpu.make_async_copy(tf_hbm, tf_ref, load_sem.at[0]),
        pltpu.make_async_copy(half_of(tp_hbm, core), half_of(pbf, core), load_sem.at[1]),
        pltpu.make_async_copy(half_of(tp_hbm, other), half_of(pbf, other), load_sem.at[2]),
        pltpu.make_async_copy(sf_hbm, sf_ref, load_sem.at[3]),
        pltpu.make_async_copy(sp_hbm, sp_ref, load_sem.at[4]),
    ]
    barrier = pltpu.get_barrier_semaphore()
    for peer in z_peers + plane_peers:
        pl.semaphore_signal(barrier, inc=1, device_id=peer, device_id_type=MESH)
    for load in loads:
        load.start()

    loads[0].wait()
    values = tf_ref[...].astype(F32)
    unit = (values * inverse_norm(jnp.sum(values * values, axis=1, keepdims=True))).astype(BF16)
    tbf[0] = unit
    tsend[...] = unit.astype(F32)

    def teacher_unit(which, j):
        at = pl.ds(pl.multiple_of(which * half + j * PART, PART), PART)
        values = pbf[:, at].astype(F32)
        return at, (values * inverse_norm(jnp.sum(values * values, axis=0, keepdims=True))).astype(BF16)

    def teacher_exp(rows, unit):
        logits = jnp.dot(tbf[rows], unit, preferred_element_type=F32)
        return jnp.exp2(logits * (math.log2(math.e) / TEACHER_TEMP))

    def own_half(j, carry):
        at, unit = teacher_unit(core, j)
        pbf[:, at] = unit
        share[core, :, pl.ds(pl.multiple_of(j * PART, PART), PART)] = teacher_exp(0, unit)
        return carry

    def far_half(j, carry):
        at, unit = teacher_unit(other, j)
        share[other, :, pl.ds(pl.multiple_of(j * PART, PART), PART)] = teacher_exp(0, unit)
        return carry

    def other_rows(j, carry):
        at = pl.ds(pl.multiple_of(j * PART, PART), PART)
        e = teacher_exp(1, pbf[:, pl.ds(pl.multiple_of(core * half + j * PART, PART), PART)])
        share[2, :, at] = e
        mass = jnp.sum(share[core, :, at], axis=0, keepdims=True) + jnp.sum(e, axis=0, keepdims=True)
        for lane in range(PART // 128):
            mass_out[0, pl.ds(j * (PART // 128) + lane, 1)] = mass[:, lane * 128 : (lane + 1) * 128]
        return carry

    loads[1].wait()
    lax.fori_loop(0, half // PART // 2, own_half, 0)
    pl.semaphore_wait(barrier, nz - 1 + plane - 1)
    teacher_copy = pltpu.make_async_remote_copy(
        tsend,
        trecv,
        ex_send.at[9],
        ex_recv.at[9],
        device_id={"batch": z * CORES + other},
        device_id_type=MESH,
    )
    teacher_copy.start()
    lax.fori_loop(half // PART // 2, half // PART, own_half, 0)
    teacher_copy.wait_recv()
    tbf[1] = trecv[...].astype(BF16)
    lax.fori_loop(0, half // PART, other_rows, 0)

    def send_mass(it):
        send(z_peers, mass_out.at[it], mass_in.at[it, z], ex_send.at[it], ex_recv.at[it])

    def send_rows(it):
        await_all(mass_in.at[it], nz, ex_recv.at[it])
        mass_in[it, pl.ds(z, 1)] = mass_out[it][None]
        col[it, core] = 1.0 / (clusters * jnp.sum(mass_in[it], axis=0))
        for which, block in ((core, core), (2, other)):

            def body(j, acc):
                at = pl.ds(pl.multiple_of(j * 128, 128), 128)
                return acc + share[which, :, at] * col[it, core, pl.ds(j, 1)]

            acc = lax.fori_loop(0, lanes, body, jnp.zeros((trows, 128), F32), unroll=4)
            for crop in range(WIDE):
                row_out[it, pl.ds(block * WIDE + crop, 1)] = jnp.sum(
                    acc[crop * images : (crop + 1) * images].T, axis=0, keepdims=True
                )
        send(plane_peers, row_out.at[it], row_in.at[it, here], ex_send.at[3 + it], ex_recv.at[3 + it])

    def row_factors(it, numerator, both):
        await_all(row_in.at[it], plane, ex_recv.at[3 + it])
        row_in[it, pl.ds(here, 1)] = row_out[it][None]
        row_inv[...] = 1.0 / jnp.sum(row_in[it], axis=0)
        for side, block in ((0, core), (1, other))[: 2 if both else 1]:
            for crop in range(WIDE):
                line = row_inv[pl.ds(block * WIDE + crop, 1)] * numerator
                rowb[side, crop * images : (crop + 1) * images] = jnp.broadcast_to(line, (128, images)).T

    def mass_of_rows(it):
        def body(j, carry):
            at = pl.ds(pl.multiple_of(j * 128, 128), 128)
            product = share[core, :, at] * rowb[0] + share[2, :, at] * rowb[1]
            mass_out[it, pl.ds(j, 1)] = jnp.sum(product, axis=0, keepdims=True)
            return carry

        lax.fori_loop(0, lanes, body, 0, unroll=2)

    def student_rows():
        loads[3].wait()

        def body(c, carry):
            first, second = carry
            at = pl.ds(pl.multiple_of(c * images, images), images)
            values = sf_ref[at, :].astype(F32)
            sraw[c] = values
            unit = (values * inverse_norm(jnp.sum(values * values, axis=1, keepdims=True))).astype(BF16)
            sbf[at, :] = unit
            wide = unit.astype(F32)
            st[:, at] = wide.T.astype(BF16)
            first = first + jnp.where(c == 0, 0.0, 1.0) * wide
            second = second + jnp.where(c == 1, 0.0, 1.0) * wide
            return first, second

        zero = jnp.zeros((images, depth), F32)
        sums = lax.fori_loop(0, crops, body, (zero, zero))
        for i, values in enumerate(sums):
            high = values.astype(BF16)
            mix[i * images : (i + 1) * images, :] = high
            mix[trows + i * images : trows + (i + 1) * images, :] = (values - high.astype(F32)).astype(BF16)
        racc[...] = jnp.zeros_like(racc)

    def student_prototypes():
        loads[4].wait()

        def body(j, carry):
            at = pl.ds(pl.multiple_of(j * PART, PART), PART)
            values = sp_ref[:, at].astype(F32)
            inverse = inverse_norm(jnp.sum(values * values, axis=0, keepdims=True))
            pscale[:, at] = inverse
            pbf[:, at] = (values * inverse).astype(BF16)
            return carry

        lax.fori_loop(0, columns // PART, body, 0)

    def student_steps(low, high):
        def body(j, carry):
            at = pl.ds(pl.multiple_of(j * WIDTH, WIDTH), WIDTH)
            block = pbf[:, at]
            e = jnp.exp2(
                jnp.dot(sbf[...], block, preferred_element_type=F32) * (math.log2(math.e) / STUDENT_TEMP)
            )
            expo[:, at] = e
            acc = racc[...]
            for lane in range(0, WIDTH, 128):
                acc = acc + e[:, lane : lane + 128]
            racc[...] = acc
            both = jnp.dot(mix[...], block, preferred_element_type=F32)
            mixed[:, at] = (both[:trows] + both[trows:]) * (1.0 / STUDENT_TEMP)
            return carry

        lax.fori_loop(low, high, body, 0)

    def send_exponentials():
        for c in range(crops):
            exp_out[c] = jnp.sum(racc[c * images : (c + 1) * images, :].T, axis=0, keepdims=True)
        send(plane_peers[: np_ - 1], exp_out, exp_in.at[p], ex_send.at[6], ex_recv.at[6])

    def student_scales():
        await_all(exp_in, np_, ex_recv.at[6])
        exp_in[pl.ds(p, 1)] = exp_out[...][None]
        for c in range(crops):
            total = jnp.sum(exp_in[:, c], axis=0)
            pairs = 1.0 if c < 2 else 2.0
            scale[c * images : (c + 1) * images, :] = jnp.broadcast_to(
                (pairs * factor) / total, (128, images)
            ).T

    send_mass(0)
    loads[2].wait()
    lax.fori_loop(0, half // PART, far_half, 0)
    student_rows()
    send_rows(0)
    student_prototypes()
    student_steps(0, steps // 8)
    row_factors(0, 1.0 / teacher_rows, True)
    mass_of_rows(1)
    send_mass(1)
    student_steps(steps // 8, steps // 2)
    send_rows(1)
    student_steps(steps // 2, steps)
    row_factors(1, 1.0 / teacher_rows, True)
    mass_of_rows(2)
    send_mass(2)
    send_exponentials()
    loss_cols[...] = jnp.zeros_like(loss_cols)
    send_rows(2)
    column_copy = pltpu.make_async_remote_copy(
        col.at[2, core],
        col.at[2, core],
        ex_send.at[10],
        ex_recv.at[10],
        device_id={"batch": z * CORES + other},
        device_id_type=MESH,
    )
    column_copy.start()
    student_scales()
    column_copy.wait_recv()

    def weigh(j, carry):
        at = pl.ds(pl.multiple_of(j * 128, 128), 128)
        for h in range(CORES):
            share[h, :, at] = share[h, :, at] * col[2, h, pl.ds(j, 1)]
        return carry

    lax.fori_loop(0, lanes, weigh, 0)
    row_factors(2, factor, False)

    def core_copy(t):
        return pltpu.make_async_remote_copy(
            wt.at[t, :, other],
            wt_core.at[t],
            core_send.at[t],
            core_recv.at[t],
            device_id={"batch": z * CORES + other},
            device_id_type=MESH,
        )

    def way_of(t, side):
        way = 1 - 2 * lax.rem(t, 2)
        return -way if side else way

    def ring_copy(t, side, s):
        way = way_of(t, side)
        segment = lax.rem(z + way * (hops[side] - s) + nz, nz)
        return pltpu.make_async_remote_copy(
            wt.at[t, segment, core],
            wt_ring.at[t, side, s],
            ring_send.at[t, side, s],
            ring_recv.at[t, side, s],
            device_id={"batch": lax.rem(z + way + nz, nz) * CORES + core},
            device_id_type=MESH,
        )

    def serve(t, phase):
        if phase == 0:
            core_copy(t).wait_recv()
            for segment in range(nz):
                wt[t, segment, pl.ds(core, 1)] += wt_core[t, pl.ds(segment, 1)]
            for side in range(2):
                if hops[side]:
                    ring_copy(t, side, 0).start()
            return
        s = phase - 1
        for side in range(2):
            if s < hops[side]:
                segment = lax.rem(z + way_of(t, side) * (hops[side] - 1 - s) + nz, nz)
                ring_copy(t, side, s).wait_recv()
                wt[t, segment, core] += wt_ring[t, side, s]
                if s + 1 < hops[side]:
                    ring_copy(t, side, s + 1).start()
        if s + 1 == hops[0]:
            at = pl.ds(pl.multiple_of(t * WIDTH, WIDTH), WIDTH)
            gp_ref[:, at] = pscale[:, at] * wt[t, z, core]

    def serve_all(k):
        for phase in range(hops[0], -1, -1):
            t = k - 1 - LAG * phase

            @pl.when(jnp.logical_and(t >= 0, t < steps))
            def _():
                serve(t, phase)

    def gradient_step(j, carry):
        at = pl.ds(pl.multiple_of(j * WIDTH, WIDTH), WIDTH)
        which = lax.div(j, steps // CORES)
        inside = pl.ds(pl.multiple_of((j - which * (steps // CORES)) * WIDTH, WIDTH), WIDTH)
        row0 = jnp.concatenate([rowb[0, :images, :]] * (WIDTH // 128), axis=1)
        row1 = jnp.concatenate([rowb[0, images:, :]] * (WIDTH // 128), axis=1)
        first = share[which, :images, inside] * row0
        second = share[which, images:, inside] * row1
        loss_cols[...] += jnp.sum(
            first * mixed[:images, at] + second * mixed[images:, at], axis=0, keepdims=True
        )
        both = first + second
        for c in range(crops):
            own_rows = slice(c * images, (c + 1) * images)
            target = second if c == 0 else first if c == 1 else both
            scales = jnp.concatenate([scale[own_rows, :]] * (WIDTH // 128), axis=1)
            grad[own_rows, at] = (expo[own_rows, at] * scales - target).astype(BF16)
        product = jnp.dot(st[...], grad[:, at], preferred_element_type=F32)
        unit = sp_ref[:, at].astype(F32) * pscale[:, at]
        curvature = jnp.sum(pbf[:, at].astype(F32) * product, axis=0, keepdims=True)
        wt[j] = (product - unit * curvature).reshape(wt.shape[1:])
        core_copy(j).start()
        serve_all(j)
        return carry

    lax.fori_loop(0, steps, gradient_step, 0)

    size = crops // GROUPS
    for group in range(GROUPS):
        low = group * size
        cot[low : low + size] = lax.dot_general(
            grad[low * images : (low + size) * images, :],
            pbf[...],
            (((1,), (1,)), ((), ())),
            preferred_element_type=F32,
        ).reshape(size, images, depth)
        for q in proto_peers:
            pltpu.make_async_remote_copy(
                cot.at[low : low + size, pl.ds(pl.multiple_of(q * own, own), own)],
                cot_in.at[group, p],
                cot_send.at[group],
                cot_recv.at[group],
                device_id={"proto": q},
                device_id_type=MESH,
            ).start()
        serve_all(steps + group)

    inverse = row_inv[...]
    portion = row_in[2, pl.ds(p, 1)] + row_in[2, pl.ds(np_ + p, 1)]
    row_inv[...] = portion[0] * inverse
    logs = [jnp.log(jnp.sum(exp_in[:, c], axis=0)) for c in range(crops)]
    shared = functools.reduce(lambda x, y: x + y, logs[2:])
    lossv = row_inv[pl.ds(core * WIDE, 1)] * (logs[1] + shared)
    lossv = lossv + row_inv[pl.ds(core * WIDE + 1, 1)] * (logs[0] + shared)
    for lane in range(0, WIDTH, 128):
        lossv = lossv - loss_cols[:, lane : lane + 128] * (1.0 / factor)
    loss_out[0] = lossv
    send(plane_peers, loss_out.at[0], loss_plane.at[here], ex_send.at[7], ex_recv.at[7])

    def tail(k, carry):
        serve_all(k)
        return carry

    middle = steps + GROUPS + LAG
    lax.fori_loop(steps + GROUPS, middle, tail, 0)
    await_all(loss_plane, plane, ex_recv.at[7])
    loss_plane[pl.ds(here, 1)] = loss_out[0][None]
    loss_out[1] = jnp.sum(loss_plane[...], axis=0)
    send(z_peers, loss_out.at[1], loss_z.at[z], ex_send.at[8], ex_recv.at[8])
    lax.fori_loop(middle, steps + LAG * hops[0] + 1, tail, 0)

    await_all(loss_z, nz, ex_recv.at[8])
    loss_z[pl.ds(z, 1)] = loss_out[1][None]
    total = jnp.sum(loss_z[...], axis=0)
    loss_ref[...] = jnp.sum(total, axis=1, keepdims=True) * (1.0 / (images_all * PAIRS))

    mine = pl.ds(pl.multiple_of(p * own, own), own)
    for group in range(GROUPS):
        low = group * size
        await_all(cot_in.at[group], np_, cot_recv.at[group])
        cot_in[group, pl.ds(p, 1)] = cot[low : low + size, mine][None]
        total = jnp.sum(cot_in[group], axis=0)
        values = sraw[low : low + size, mine]
        inverse = inverse_norm(jnp.sum(values * values, axis=2, keepdims=True))
        unit = values * inverse
        gf_ref[low : low + size] = inverse * (total - unit * jnp.sum(unit * total, axis=2, keepdims=True))

    for it in range(SK_ITERS):
        await_all(mass_in.at[it], nz, ex_send.at[it])
        await_all(row_in.at[it], plane, ex_send.at[3 + it])
    await_all(exp_in, np_, ex_send.at[6])
    await_all(loss_plane, plane, ex_send.at[7])
    await_all(loss_z, nz, ex_send.at[8])
    teacher_copy.wait_send()
    column_copy.wait_send()
    for group in range(GROUPS):
        await_all(cot_in.at[group], np_, cot_send.at[group])

    def sent(t, carry):
        core_copy(t).wait_send()
        for side in range(2):
            for s in range(hops[side]):
                ring_copy(t, side, s).wait_send()
        return carry

    lax.fori_loop(0, steps, sent, 0)


def on_device(student_features, teacher_features, student_prototypes, teacher_prototypes):
    crops, images, depth = student_features.shape
    columns = student_prototypes.shape[1]
    nb, np_ = lax.axis_size("batch"), lax.axis_size("proto")
    nz = nb // CORES
    rows, trows = crops * images, WIDE * images
    steps, deep, half = columns // WIDTH, depth // nb, columns // CORES
    lanes, own = half // 128, images // np_
    vmem = pltpu.VMEM
    dma = pltpu.SemaphoreType.DMA
    loss, grad_features, grad_prototypes = pl.pallas_call(
        functools.partial(kernel, nb, np_),
        out_shape=(
            jax.ShapeDtypeStruct((1, 1), F32),
            jax.ShapeDtypeStruct((crops, own, depth), F32),
            jax.ShapeDtypeStruct((deep, columns), F32),
        ),
        in_specs=[pl.BlockSpec(memory_space=pl.ANY)] * 4,
        out_specs=[pl.BlockSpec(memory_space=vmem)] * 3,
        scratch_shapes=[
            vmem((rows, depth), BF16),
            vmem((trows, depth), BF16),
            vmem((depth, columns), BF16),
            vmem((depth, columns), BF16),
            vmem((2, trows, depth), BF16),
            vmem((trows, depth), F32),
            vmem((trows, depth), F32),
            vmem((3, trows, half), F32),
            vmem((rows, columns), F32),
            vmem((trows, columns), F32),
            vmem((crops, images, depth), F32),
            vmem((rows, depth), BF16),
            vmem((depth, rows), BF16),
            vmem((2 * trows, depth), BF16),
            vmem((1, columns), F32),
            vmem((rows, 128), F32),
            vmem((rows, 128), F32),
            vmem((rows, columns), BF16),
            vmem((crops, images, depth), F32),
            vmem((GROUPS, np_, crops // GROUPS, own, depth), F32),
            vmem((steps, nz, CORES, deep, WIDTH), F32),
            vmem((steps, nz, deep, WIDTH), F32),
            vmem((steps, 2, nz // 2, deep, WIDTH), F32),
            vmem((2, trows, 128), F32),
            vmem((SK_ITERS, lanes, 128), F32),
            vmem((SK_ITERS, nz, lanes, 128), F32),
            vmem((SK_ITERS, CORES, lanes, 128), F32),
            vmem((SK_ITERS, CORES * WIDE, 128), F32),
            vmem((SK_ITERS, CORES * np_, CORES * WIDE, 128), F32),
            vmem((CORES * WIDE, 128), F32),
            vmem((crops, 1, images), F32),
            vmem((np_, crops, 1, images), F32),
            vmem((1, WIDTH), F32),
            vmem((2, 1, 128), F32),
            vmem((CORES * np_, 1, 128), F32),
            vmem((nz, 1, 128), F32),
            dma((5,)),
            dma((11,)),
            dma((11,)),
            dma((GROUPS,)),
            dma((GROUPS,)),
            dma((steps,)),
            dma((steps,)),
            dma((steps, 2, nz // 2)),
            dma((steps, 2, nz // 2)),
        ],
        compiler_params=pltpu.CompilerParams(
            collective_id=0, has_side_effects=True, vmem_limit_bytes=63 * 1024 * 1024
        ),
    )(
        student_features.reshape(rows, depth),
        teacher_features.reshape(trows, depth),
        student_prototypes,
        teacher_prototypes,
    )
    return loss[0, 0], grad_features, grad_prototypes


def solution(mesh):
    return jax.shard_map(
        on_device,
        mesh=mesh,
        in_specs=(P(None, "batch", None), P(None, "batch", None), P(None, "proto"), P(None, "proto")),
        out_specs=(P(), P(None, ("batch", "proto"), None), P("batch", "proto")),
        check_vma=False,
    )
```

```python
import functools
import math

import jax
import jax.numpy as jnp
from jax import lax
from jax.experimental import pallas as pl
from jax.experimental.pallas import tpu as pltpu
from jax.sharding import PartitionSpec as P

WIDE = 2
SK_ITERS = 3
PAIRS = 18
CORES = 2
STUDENT_TEMP = 0.1
TEACHER_TEMP = 0.07
NORM_EPS = 1e-06
MESH = pl.DeviceIdType.MESH
F32 = jnp.float32
BF16 = jnp.bfloat16
WIDTH = 512
PART = 256
LAG = 4
GROUPS = 2
BURST = 3
EACH = 5


def inverse_norm(squares):
    return lax.rsqrt(squares + NORM_EPS)


def kernel(
    nb,
    np_,
    sf_hbm,
    tf_hbm,
    sp_hbm,
    tp_hbm,
    loss_ref,
    gf_ref,
    gp_ref,
    sf_ref,
    tf_ref,
    sp_ref,
    pbf,
    tbf,
    tsend,
    trecv,
    share,
    expo,
    mixed,
    sraw,
    sbf,
    st,
    mix,
    pscale,
    racc,
    scale,
    grad,
    cot,
    cot_in,
    wt,
    wt_core,
    wt_ring,
    rowb,
    mass_out,
    mass_in,
    col,
    row_out,
    row_in,
    row_inv,
    exp_out,
    exp_in,
    loss_cols,
    loss_out,
    loss_plane,
    loss_z,
    load_sem,
    ex_send,
    ex_recv,
    cot_send,
    cot_recv,
    core_send,
    core_recv,
    ring_send,
    ring_recv,
):
    b = lax.axis_index("batch")
    p = lax.axis_index("proto")
    nz = nb // CORES
    z, core = lax.div(b, CORES), lax.rem(b, CORES)
    other = 1 - core
    half = share.shape[2]
    lanes = half // 128
    columns = CORES * half
    crops, images, depth = sraw.shape
    steps = columns // WIDTH
    own = images // np_
    images_all = images * nb
    teacher_rows = WIDE * images_all
    clusters = columns * np_
    factor = 1.0 / (images_all * PAIRS * STUDENT_TEMP)
    trows = WIDE * images
    plane = CORES * np_
    here = core * np_ + p
    hops = (nz // 2, nz - 1 - nz // 2)

    far = sorted(range(1, nz), key=lambda k: -min(k, nz - k))
    z_peers = [{"batch": lax.rem(z + k, nz) * CORES + core} for k in far]
    side = math.isqrt(np_)
    y, x = lax.div(p, side), lax.rem(p, side)
    offsets = [(dy, dx) for dy in range(np_ // side) for dx in range(side)][1:]
    offsets.sort(key=lambda o: -min(o[0], np_ // side - o[0]) - min(o[1], side - o[1]))
    proto_peers = [lax.rem(y + dy, np_ // side) * side + lax.rem(x + dx, side) for dy, dx in offsets]
    plane_peers = []
    for q in proto_peers:
        plane_peers += [{"batch": z * CORES + other, "proto": q}, {"proto": q}]
    plane_peers += [{"batch": z * CORES + other}]

    def send(peers, source, target, sends, receives):
        for peer in peers:
            pltpu.make_async_remote_copy(
                source, target, sends, receives, device_id=peer, device_id_type=MESH
            ).start()

    def await_all(block, n, sem):
        view = block.at[pl.ds(0, n - 1)]
        pltpu.make_async_copy(view, view, sem).wait()

    def half_of(ref, which):
        return ref.at[:, pl.ds(pl.multiple_of(which * half, half), half)]

    loads = [
        pltpu.make_async_copy(tf_hbm, tf_ref, load_sem.at[0]),
        pltpu.make_async_copy(half_of(tp_hbm, core), half_of(pbf, core), load_sem.at[1]),
        pltpu.make_async_copy(half_of(tp_hbm, other), half_of(pbf, other), load_sem.at[2]),
        pltpu.make_async_copy(sf_hbm, sf_ref, load_sem.at[3]),
        pltpu.make_async_copy(sp_hbm, sp_ref, load_sem.at[4]),
    ]
    barrier = pltpu.get_barrier_semaphore()
    for peer in z_peers + plane_peers:
        pl.semaphore_signal(barrier, inc=1, device_id=peer, device_id_type=MESH)
    for load in loads:
        load.start()

    loads[0].wait()
    values = tf_ref[...].astype(F32)
    unit = (values * inverse_norm(jnp.sum(values * values, axis=1, keepdims=True))).astype(BF16)
    tbf[0] = unit
    tsend[...] = unit.astype(F32)

    def teacher_unit(which, j):
        at = pl.ds(pl.multiple_of(which * half + j * PART, PART), PART)
        values = pbf[:, at].astype(F32)
        return at, (values * inverse_norm(jnp.sum(values * values, axis=0, keepdims=True))).astype(BF16)

    def teacher_exp(rows, unit):
        logits = jnp.dot(tbf[rows], unit, preferred_element_type=F32)
        return jnp.exp2(logits * (math.log2(math.e) / TEACHER_TEMP))

    def own_half(j, carry):
        at, unit = teacher_unit(core, j)
        pbf[:, at] = unit
        share[core, :, pl.ds(pl.multiple_of(j * PART, PART), PART)] = teacher_exp(0, unit)
        return carry

    def far_half(j, carry):
        at, unit = teacher_unit(other, j)
        share[other, :, pl.ds(pl.multiple_of(j * PART, PART), PART)] = teacher_exp(0, unit)
        return carry

    def other_rows(j, carry):
        at = pl.ds(pl.multiple_of(j * PART, PART), PART)
        e = teacher_exp(1, pbf[:, pl.ds(pl.multiple_of(core * half + j * PART, PART), PART)])
        share[2, :, at] = e
        mass = jnp.sum(share[core, :, at], axis=0, keepdims=True) + jnp.sum(e, axis=0, keepdims=True)
        for lane in range(PART // 128):
            mass_out[0, pl.ds(j * (PART // 128) + lane, 1)] = mass[:, lane * 128 : (lane + 1) * 128]
        return carry

    loads[1].wait()
    lax.fori_loop(0, half // PART // 2, own_half, 0)
    pl.semaphore_wait(barrier, nz - 1 + plane - 1)
    teacher_copy = pltpu.make_async_remote_copy(
        tsend,
        trecv,
        ex_send.at[9],
        ex_recv.at[9],
        device_id={"batch": z * CORES + other},
        device_id_type=MESH,
    )
    teacher_copy.start()
    lax.fori_loop(half // PART // 2, half // PART, own_half, 0)
    teacher_copy.wait_recv()
    tbf[1] = trecv[...].astype(BF16)
    lax.fori_loop(0, half // PART, other_rows, 0)

    def send_mass(it):
        send(z_peers, mass_out.at[it], mass_in.at[it, z], ex_send.at[it], ex_recv.at[it])

    def send_rows(it):
        await_all(mass_in.at[it], nz, ex_recv.at[it])
        mass_in[it, pl.ds(z, 1)] = mass_out[it][None]
        col[it, core] = 1.0 / (clusters * jnp.sum(mass_in[it], axis=0))
        for which, block in ((core, core), (2, other)):

            def body(j, acc):
                at = pl.ds(pl.multiple_of(j * 128, 128), 128)
                return acc + share[which, :, at] * col[it, core, pl.ds(j, 1)]

            acc = lax.fori_loop(0, lanes, body, jnp.zeros((trows, 128), F32), unroll=4)
            for crop in range(WIDE):
                row_out[it, pl.ds(block * WIDE + crop, 1)] = jnp.sum(
                    acc[crop * images : (crop + 1) * images].T, axis=0, keepdims=True
                )
        send(plane_peers, row_out.at[it], row_in.at[it, here], ex_send.at[3 + it], ex_recv.at[3 + it])

    def row_factors(it, numerator, both):
        await_all(row_in.at[it], plane, ex_recv.at[3 + it])
        row_in[it, pl.ds(here, 1)] = row_out[it][None]
        row_inv[...] = 1.0 / jnp.sum(row_in[it], axis=0)
        for side, block in ((0, core), (1, other))[: 2 if both else 1]:
            for crop in range(WIDE):
                line = row_inv[pl.ds(block * WIDE + crop, 1)] * numerator
                rowb[side, crop * images : (crop + 1) * images] = jnp.broadcast_to(line, (128, images)).T

    def mass_of_rows(it):
        def body(j, carry):
            at = pl.ds(pl.multiple_of(j * 128, 128), 128)
            product = share[core, :, at] * rowb[0] + share[2, :, at] * rowb[1]
            mass_out[it, pl.ds(j, 1)] = jnp.sum(product, axis=0, keepdims=True)
            return carry

        lax.fori_loop(0, lanes, body, 0, unroll=2)

    def student_rows():
        loads[3].wait()

        def body(c, carry):
            first, second = carry
            at = pl.ds(pl.multiple_of(c * images, images), images)
            values = sf_ref[at, :].astype(F32)
            sraw[c] = values
            unit = (values * inverse_norm(jnp.sum(values * values, axis=1, keepdims=True))).astype(BF16)
            sbf[at, :] = unit
            wide = unit.astype(F32)
            st[:, at] = wide.T.astype(BF16)
            first = first + jnp.where(c == 0, 0.0, 1.0) * wide
            second = second + jnp.where(c == 1, 0.0, 1.0) * wide
            return first, second

        zero = jnp.zeros((images, depth), F32)
        sums = lax.fori_loop(0, crops, body, (zero, zero))
        for i, values in enumerate(sums):
            high = values.astype(BF16)
            mix[i * images : (i + 1) * images, :] = high
            mix[trows + i * images : trows + (i + 1) * images, :] = (values - high.astype(F32)).astype(BF16)
        racc[...] = jnp.zeros_like(racc)

    def student_prototypes():
        loads[4].wait()

        def body(j, carry):
            at = pl.ds(pl.multiple_of(j * PART, PART), PART)
            values = sp_ref[:, at].astype(F32)
            inverse = inverse_norm(jnp.sum(values * values, axis=0, keepdims=True))
            pscale[:, at] = inverse
            pbf[:, at] = (values * inverse).astype(BF16)
            return carry

        lax.fori_loop(0, columns // PART, body, 0)

    def student_steps(low, high):
        def body(j, carry):
            at = pl.ds(pl.multiple_of(j * WIDTH, WIDTH), WIDTH)
            block = pbf[:, at]
            e = jnp.exp2(
                jnp.dot(sbf[...], block, preferred_element_type=F32) * (math.log2(math.e) / STUDENT_TEMP)
            )
            expo[:, at] = e
            acc = racc[...]
            for lane in range(0, WIDTH, 128):
                acc = acc + e[:, lane : lane + 128]
            racc[...] = acc
            both = jnp.dot(mix[...], block, preferred_element_type=F32)
            mixed[:, at] = (both[:trows] + both[trows:]) * (1.0 / STUDENT_TEMP)
            return carry

        lax.fori_loop(low, high, body, 0)

    def send_exponentials():
        for c in range(crops):
            exp_out[c] = jnp.sum(racc[c * images : (c + 1) * images, :].T, axis=0, keepdims=True)
        send([{"proto": q} for q in proto_peers], exp_out, exp_in.at[p], ex_send.at[6], ex_recv.at[6])

    def student_scales():
        await_all(exp_in, np_, ex_recv.at[6])
        exp_in[pl.ds(p, 1)] = exp_out[...][None]
        for c in range(crops):
            total = jnp.sum(exp_in[:, c], axis=0)
            pairs = 1.0 if c < 2 else 2.0
            scale[c * images : (c + 1) * images, :] = jnp.broadcast_to(
                (pairs * factor) / total, (128, images)
            ).T

        def body(j, carry):
            at = pl.ds(pl.multiple_of(j * 128, 128), 128)
            expo[:, at] = expo[:, at] * scale[...]
            return carry

        lax.fori_loop(0, columns // 128, body, 0)

    send_mass(0)
    loads[2].wait()
    lax.fori_loop(0, half // PART, far_half, 0)
    student_rows()
    send_rows(0)
    student_prototypes()
    student_steps(0, steps // 8)
    row_factors(0, 1.0 / teacher_rows, True)
    mass_of_rows(1)
    send_mass(1)
    student_steps(steps // 8, steps // 2)
    send_rows(1)
    student_steps(steps // 2, steps)
    row_factors(1, 1.0 / teacher_rows, True)
    mass_of_rows(2)
    send_mass(2)
    send_exponentials()
    loss_cols[...] = jnp.zeros_like(loss_cols)
    send_rows(2)
    column_copy = pltpu.make_async_remote_copy(
        col.at[2, core],
        col.at[2, core],
        ex_send.at[10],
        ex_recv.at[10],
        device_id={"batch": z * CORES + other},
        device_id_type=MESH,
    )
    column_copy.start()
    student_scales()
    column_copy.wait_recv()

    def weigh(j, carry):
        at = pl.ds(pl.multiple_of(j * 128, 128), 128)
        for h in range(CORES):
            share[h, :, at] = share[h, :, at] * col[2, h, pl.ds(j, 1)]
        return carry

    lax.fori_loop(0, lanes, weigh, 0)
    row_factors(2, factor, False)

    def core_copy(t):
        return pltpu.make_async_remote_copy(
            wt.at[t, :, other],
            wt_core.at[t],
            core_send.at[t],
            core_recv.at[t],
            device_id={"batch": z * CORES + other},
            device_id_type=MESH,
        )

    def way_of(t, side):
        way = 1 - 2 * lax.rem(t, 2)
        return -way if side else way

    def ring_copy(t, side, s):
        way = way_of(t, side)
        segment = lax.rem(z + way * (hops[side] - s) + nz, nz)
        return pltpu.make_async_remote_copy(
            wt.at[t, segment, core],
            wt_ring.at[t, side, s],
            ring_send.at[t, side, s],
            ring_recv.at[t, side, s],
            device_id={"batch": lax.rem(z + way + nz, nz) * CORES + core},
            device_id_type=MESH,
        )

    def serve(t, phase):
        if phase == 0:
            core_copy(t).wait_recv()
            for segment in range(nz):
                wt[t, segment, pl.ds(core, 1)] += wt_core[t, pl.ds(segment, 1)]
            for side in range(2):
                if hops[side]:
                    ring_copy(t, side, 0).start()
            return
        s = phase - 1
        for side in range(2):
            if s < hops[side]:
                segment = lax.rem(z + way_of(t, side) * (hops[side] - 1 - s) + nz, nz)
                ring_copy(t, side, s).wait_recv()
                wt[t, segment, core] += wt_ring[t, side, s]
                if s + 1 < hops[side]:
                    ring_copy(t, side, s + 1).start()
        if s + 1 == hops[0]:
            at = pl.ds(pl.multiple_of(t * WIDTH, WIDTH), WIDTH)
            gp_ref[:, at] = pscale[:, at] * wt[t, z, core]

    def serve_all(k):
        for phase in range(hops[0], -1, -1):
            t = k - 1 - LAG * phase

            @pl.when(jnp.logical_and(t >= 0, t < steps))
            def _():
                serve(t, phase)

    def gradient_step(j, carry):
        at = pl.ds(pl.multiple_of(j * WIDTH, WIDTH), WIDTH)
        which = lax.div(j, steps // CORES)
        inside = pl.ds(pl.multiple_of((j - which * (steps // CORES)) * WIDTH, WIDTH), WIDTH)
        row0 = jnp.concatenate([rowb[0, :images, :]] * (WIDTH // 128), axis=1)
        row1 = jnp.concatenate([rowb[0, images:, :]] * (WIDTH // 128), axis=1)
        first = share[which, :images, inside] * row0
        second = share[which, images:, inside] * row1
        loss_cols[...] += jnp.sum(
            first * mixed[:images, at] + second * mixed[images:, at], axis=0, keepdims=True
        )
        both = first + second
        for c in range(crops):
            own_rows = slice(c * images, (c + 1) * images)
            target = second if c == 0 else first if c == 1 else both
            grad[own_rows, at] = (expo[own_rows, at] - target).astype(BF16)
        product = jnp.dot(st[...], grad[:, at], preferred_element_type=F32)
        unit = sp_ref[:, at].astype(F32) * pscale[:, at]
        curvature = jnp.sum(pbf[:, at].astype(F32) * product, axis=0, keepdims=True)
        wt[j] = (product - unit * curvature).reshape(wt.shape[1:])
        core_copy(j).start()
        serve_all(j)
        return carry

    lax.fori_loop(0, steps, gradient_step, 0)

    size = crops // GROUPS

    def send_cot(i):
        group = lax.div(i, np_ - 1)
        q = lax.rem(p + 1 + lax.rem(i, np_ - 1), np_)
        pltpu.make_async_remote_copy(
            cot.at[
                pl.ds(group * size, size), pl.ds(pl.multiple_of(q * own, own), own)
            ],
            cot_in.at[group, p],
            cot_send.at[group],
            cot_recv.at[group],
            device_id={"proto": q},
            device_id_type=MESH,
        ).start()

    def send_more(k):
        rest = max(np_ - 1 - BURST, 0)
        for u in range(EACH):
            n = (k - steps - GROUPS) * EACH + u

            @pl.when(n < GROUPS * rest)
            def _():
                send_cot(lax.div(n, rest) * (np_ - 1) + BURST + lax.rem(n, rest))

    for group in range(GROUPS):
        low = group * size
        cot[low : low + size] = lax.dot_general(
            grad[low * images : (low + size) * images, :],
            pbf[...],
            (((1,), (1,)), ((), ())),
            preferred_element_type=F32,
        ).reshape(size, images, depth)
        for k in range(min(BURST, np_ - 1)):
            send_cot(group * (np_ - 1) + k)
        serve_all(steps + group)

    inverse = row_inv[...]
    portion = row_in[2, pl.ds(p, 1)] + row_in[2, pl.ds(np_ + p, 1)]
    row_inv[...] = portion[0] * inverse
    logs = [jnp.log(jnp.sum(exp_in[:, c], axis=0)) for c in range(crops)]
    shared = functools.reduce(lambda x, y: x + y, logs[2:])
    lossv = row_inv[pl.ds(core * WIDE, 1)] * (logs[1] + shared)
    lossv = lossv + row_inv[pl.ds(core * WIDE + 1, 1)] * (logs[0] + shared)
    for lane in range(0, WIDTH, 128):
        lossv = lossv - loss_cols[:, lane : lane + 128] * (1.0 / factor)
    loss_out[0] = lossv
    send(plane_peers, loss_out.at[0], loss_plane.at[here], ex_send.at[7], ex_recv.at[7])

    def tail(k, carry):
        serve_all(k)
        if np_ - 1 > BURST:
            send_more(k)
        return carry

    middle = steps + GROUPS + LAG
    lax.fori_loop(steps + GROUPS, middle, tail, 0)
    await_all(loss_plane, plane, ex_recv.at[7])
    loss_plane[pl.ds(here, 1)] = loss_out[0][None]
    loss_out[1] = jnp.sum(loss_plane[...], axis=0)
    send(z_peers, loss_out.at[1], loss_z.at[z], ex_send.at[8], ex_recv.at[8])
    lax.fori_loop(middle, steps + LAG * hops[0] + 1, tail, 0)

    await_all(loss_z, nz, ex_recv.at[8])
    loss_z[pl.ds(z, 1)] = loss_out[1][None]
    total = jnp.sum(loss_z[...], axis=0)
    loss_ref[...] = jnp.sum(total, axis=1, keepdims=True) * (1.0 / (images_all * PAIRS))

    mine = pl.ds(pl.multiple_of(p * own, own), own)
    for group in range(GROUPS):
        low = group * size
        await_all(cot_in.at[group], np_, cot_recv.at[group])
        cot_in[group, pl.ds(p, 1)] = cot[low : low + size, mine][None]
        total = jnp.sum(cot_in[group], axis=0)
        values = sraw[low : low + size, mine]
        inverse = inverse_norm(jnp.sum(values * values, axis=2, keepdims=True))
        unit = values * inverse
        gf_ref[low : low + size] = inverse * (total - unit * jnp.sum(unit * total, axis=2, keepdims=True))

    for it in range(SK_ITERS):
        await_all(mass_in.at[it], nz, ex_send.at[it])
        await_all(row_in.at[it], plane, ex_send.at[3 + it])
    await_all(exp_in, np_, ex_send.at[6])
    await_all(loss_plane, plane, ex_send.at[7])
    await_all(loss_z, nz, ex_send.at[8])
    teacher_copy.wait_send()
    column_copy.wait_send()
    for group in range(GROUPS):
        await_all(cot_in.at[group], np_, cot_send.at[group])

    def sent(t, carry):
        core_copy(t).wait_send()
        for side in range(2):
            for s in range(hops[side]):
                ring_copy(t, side, s).wait_send()
        return carry

    lax.fori_loop(0, steps, sent, 0)


def hand_on(*refs):
    for source, target in zip(refs[:3], refs[3:]):
        target[...] = source[...]


def on_device(student_features, teacher_features, student_prototypes, teacher_prototypes):
    crops, images, depth = student_features.shape
    columns = student_prototypes.shape[1]
    nb, np_ = lax.axis_size("batch"), lax.axis_size("proto")
    nz = nb // CORES
    rows, trows = crops * images, WIDE * images
    steps, deep, half = columns // WIDTH, depth // nb, columns // CORES
    lanes, own = half // 128, images // np_
    vmem = pltpu.VMEM
    dma = pltpu.SemaphoreType.DMA
    loss, grad_features, grad_prototypes = pl.pallas_call(
        functools.partial(kernel, nb, np_),
        out_shape=(
            jax.ShapeDtypeStruct((1, 1), F32),
            jax.ShapeDtypeStruct((crops, own, depth), F32),
            jax.ShapeDtypeStruct((deep, columns), F32),
        ),
        in_specs=[pl.BlockSpec(memory_space=pl.ANY)] * 4,
        out_specs=[pl.BlockSpec(memory_space=vmem)] * 3,
        scratch_shapes=[
            vmem((rows, depth), BF16),
            vmem((trows, depth), BF16),
            vmem((depth, columns), BF16),
            vmem((depth, columns), BF16),
            vmem((2, trows, depth), BF16),
            vmem((trows, depth), F32),
            vmem((trows, depth), F32),
            vmem((3, trows, half), F32),
            vmem((rows, columns), F32),
            vmem((trows, columns), F32),
            vmem((crops, images, depth), F32),
            vmem((rows, depth), BF16),
            vmem((depth, rows), BF16),
            vmem((2 * trows, depth), BF16),
            vmem((1, columns), F32),
            vmem((rows, 128), F32),
            vmem((rows, 128), F32),
            vmem((rows, columns), BF16),
            vmem((crops, images, depth), F32),
            vmem((GROUPS, np_, crops // GROUPS, own, depth), F32),
            vmem((steps, nz, CORES, deep, WIDTH), F32),
            vmem((steps, nz, deep, WIDTH), F32),
            vmem((steps, 2, nz // 2, deep, WIDTH), F32),
            vmem((2, trows, 128), F32),
            vmem((SK_ITERS, lanes, 128), F32),
            vmem((SK_ITERS, nz, lanes, 128), F32),
            vmem((SK_ITERS, CORES, lanes, 128), F32),
            vmem((SK_ITERS, CORES * WIDE, 128), F32),
            vmem((SK_ITERS, CORES * np_, CORES * WIDE, 128), F32),
            vmem((CORES * WIDE, 128), F32),
            vmem((crops, 1, images), F32),
            vmem((np_, crops, 1, images), F32),
            vmem((1, WIDTH), F32),
            vmem((2, 1, 128), F32),
            vmem((CORES * np_, 1, 128), F32),
            vmem((nz, 1, 128), F32),
            dma((5,)),
            dma((11,)),
            dma((11,)),
            dma((GROUPS,)),
            dma((GROUPS,)),
            dma((steps,)),
            dma((steps,)),
            dma((steps, 2, nz // 2)),
            dma((steps, 2, nz // 2)),
        ],
        compiler_params=pltpu.CompilerParams(
            collective_id=0, has_side_effects=True, vmem_limit_bytes=63 * 1024 * 1024
        ),
    )(
        student_features.reshape(rows, depth),
        teacher_features.reshape(trows, depth),
        student_prototypes,
        teacher_prototypes,
    )
    loss, grad_features, grad_prototypes = pl.pallas_call(
        hand_on,
        out_shape=[jax.ShapeDtypeStruct(r.shape, r.dtype) for r in (loss, grad_features, grad_prototypes)],
        in_specs=[pl.BlockSpec(memory_space=vmem)] * 3,
        out_specs=[pl.BlockSpec(memory_space=vmem)] * 3,
    )(loss, grad_features, grad_prototypes)
    return loss[0, 0], grad_features, grad_prototypes


def solution(mesh):
    return jax.shard_map(
        on_device,
        mesh=mesh,
        in_specs=(P(None, "batch", None), P(None, "batch", None), P(None, "proto"), P(None, "proto")),
        out_specs=(P(), P(None, ("batch", "proto"), None), P("batch", "proto")),
        check_vma=False,
    )
```

```python
import functools
import math

import jax
import jax.numpy as jnp
from jax import lax
from jax.experimental import pallas as pl
from jax.experimental.pallas import tpu as pltpu
from jax.sharding import PartitionSpec as P

WIDE = 2
SK_ITERS = 3
PAIRS = 18
CORES = 2
STUDENT_TEMP = 0.1
TEACHER_TEMP = 0.07
NORM_EPS = 1e-06
MESH = pl.DeviceIdType.MESH
F32 = jnp.float32
BF16 = jnp.bfloat16
WIDTH = 512
PART = 256
FIRST = 2
LAG = 3
GROUPS = 2
BURST = 3
EACH = 5


def inverse_norm(squares):
    return lax.rsqrt(squares + NORM_EPS)


def kernel(
    nb,
    np_,
    sf_hbm,
    tf_hbm,
    sp_hbm,
    tp_hbm,
    loss_ref,
    gf_ref,
    gp_ref,
    sf_ref,
    tf_ref,
    sp_ref,
    pbf,
    tbf,
    tsend,
    trecv,
    share,
    expo,
    mixed,
    sraw,
    sbf,
    st,
    mix,
    pscale,
    racc,
    scale,
    grad,
    cot,
    cot_in,
    wt,
    wt_core,
    wt_ring,
    rowb,
    mass_out,
    mass_in,
    col,
    row_out,
    row_in,
    row_inv,
    exp_out,
    exp_in,
    loss_cols,
    loss_out,
    loss_plane,
    loss_z,
    load_sem,
    ex_send,
    ex_recv,
    cot_send,
    cot_recv,
    core_send,
    core_recv,
    ring_send,
    ring_recv,
):
    b = lax.axis_index("batch")
    p = lax.axis_index("proto")
    nz = nb // CORES
    z, core = lax.div(b, CORES), lax.rem(b, CORES)
    other = 1 - core
    half = share.shape[2]
    lanes = half // 128
    columns = CORES * half
    crops, images, depth = sraw.shape
    steps = columns // WIDTH
    own = images // np_
    images_all = images * nb
    teacher_rows = WIDE * images_all
    clusters = columns * np_
    factor = 1.0 / (images_all * PAIRS * STUDENT_TEMP)
    trows = WIDE * images
    plane = CORES * np_
    here = core * np_ + p
    hops = (nz // 2, nz - 1 - nz // 2)

    far = sorted(range(1, nz), key=lambda k: -min(k, nz - k))
    z_peers = [{"batch": lax.rem(z + k, nz) * CORES + core} for k in far]
    side = math.isqrt(np_)
    y, x = lax.div(p, side), lax.rem(p, side)
    offsets = [(dy, dx) for dy in range(np_ // side) for dx in range(side)][1:]
    offsets.sort(key=lambda o: -min(o[0], np_ // side - o[0]) - min(o[1], side - o[1]))
    proto_peers = [lax.rem(y + dy, np_ // side) * side + lax.rem(x + dx, side) for dy, dx in offsets]
    plane_peers = []
    for q in proto_peers:
        plane_peers += [{"batch": z * CORES + other, "proto": q}, {"proto": q}]
    plane_peers += [{"batch": z * CORES + other}]

    def send(peers, source, target, sends, receives):
        for peer in peers:
            pltpu.make_async_remote_copy(
                source, target, sends, receives, device_id=peer, device_id_type=MESH
            ).start()

    def await_all(block, n, sem):
        view = block.at[pl.ds(0, n - 1)]
        pltpu.make_async_copy(view, view, sem).wait()

    def half_of(ref, which):
        return ref.at[:, pl.ds(pl.multiple_of(which * half, half), half)]

    loads = [
        pltpu.make_async_copy(tf_hbm, tf_ref, load_sem.at[0]),
        pltpu.make_async_copy(half_of(tp_hbm, core), half_of(pbf, core), load_sem.at[1]),
        pltpu.make_async_copy(half_of(tp_hbm, other), half_of(pbf, other), load_sem.at[2]),
        pltpu.make_async_copy(sf_hbm, sf_ref, load_sem.at[3]),
        pltpu.make_async_copy(sp_hbm, sp_ref, load_sem.at[4]),
    ]
    barrier = pltpu.get_barrier_semaphore()
    for load in loads:
        load.start()
    for peer in z_peers + plane_peers:
        pl.semaphore_signal(barrier, inc=1, device_id=peer, device_id_type=MESH)

    loads[0].wait()
    values = tf_ref[...].astype(F32)
    unit = (values * inverse_norm(jnp.sum(values * values, axis=1, keepdims=True))).astype(BF16)
    tbf[0] = unit
    tsend[...] = unit.astype(F32)

    def teacher_unit(which, j):
        at = pl.ds(pl.multiple_of(which * half + j * PART, PART), PART)
        values = pbf[:, at].astype(F32)
        return at, (values * inverse_norm(jnp.sum(values * values, axis=0, keepdims=True))).astype(BF16)

    def teacher_exp(rows, unit):
        logits = jnp.dot(tbf[rows], unit, preferred_element_type=F32)
        return jnp.exp2(logits * (math.log2(math.e) / TEACHER_TEMP))

    def own_half(j, carry):
        at, unit = teacher_unit(core, j)
        pbf[:, at] = unit
        share[core, :, pl.ds(pl.multiple_of(j * PART, PART), PART)] = teacher_exp(0, unit)
        return carry

    def far_half(j, carry):
        at, unit = teacher_unit(other, j)
        share[other, :, pl.ds(pl.multiple_of(j * PART, PART), PART)] = teacher_exp(0, unit)
        return carry

    def other_rows(j, carry):
        at = pl.ds(pl.multiple_of(j * PART, PART), PART)
        e = teacher_exp(1, pbf[:, pl.ds(pl.multiple_of(core * half + j * PART, PART), PART)])
        share[2, :, at] = e
        mass = jnp.sum(share[core, :, at], axis=0, keepdims=True) + jnp.sum(e, axis=0, keepdims=True)
        for lane in range(PART // 128):
            mass_out[0, pl.ds(j * (PART // 128) + lane, 1)] = mass[:, lane * 128 : (lane + 1) * 128]
        return carry

    pl.semaphore_wait(barrier, nz - 1 + plane - 1)
    teacher_copy = pltpu.make_async_remote_copy(
        tsend,
        trecv,
        ex_send.at[9],
        ex_recv.at[9],
        device_id={"batch": z * CORES + other},
        device_id_type=MESH,
    )
    teacher_copy.start()
    loads[1].wait()
    lax.fori_loop(0, half // PART, own_half, 0)
    teacher_copy.wait_recv()
    tbf[1] = trecv[...].astype(BF16)
    lax.fori_loop(0, half // PART, other_rows, 0)

    def send_mass(it):
        send(z_peers, mass_out.at[it], mass_in.at[it, z], ex_send.at[it], ex_recv.at[it])

    def send_rows(it):
        await_all(mass_in.at[it], nz, ex_recv.at[it])
        mass_in[it, pl.ds(z, 1)] = mass_out[it][None]
        col[it, core] = 1.0 / (clusters * jnp.sum(mass_in[it], axis=0))
        for which, block in ((core, core), (2, other)):

            def body(j, acc):
                at = pl.ds(pl.multiple_of(j * 128, 128), 128)
                return acc + share[which, :, at] * col[it, core, pl.ds(j, 1)]

            acc = lax.fori_loop(0, lanes, body, jnp.zeros((trows, 128), F32), unroll=4)
            for crop in range(WIDE):
                row_out[it, pl.ds(block * WIDE + crop, 1)] = jnp.sum(
                    acc[crop * images : (crop + 1) * images].T, axis=0, keepdims=True
                )
        send(plane_peers, row_out.at[it], row_in.at[it, here], ex_send.at[3 + it], ex_recv.at[3 + it])

    def row_factors(it, numerator, both):
        await_all(row_in.at[it], plane, ex_recv.at[3 + it])
        row_in[it, pl.ds(here, 1)] = row_out[it][None]
        row_inv[...] = 1.0 / jnp.sum(row_in[it], axis=0)
        for side, block in ((0, core), (1, other))[: 2 if both else 1]:
            for crop in range(WIDE):
                line = row_inv[pl.ds(block * WIDE + crop, 1)] * numerator
                rowb[side, crop * images : (crop + 1) * images] = jnp.broadcast_to(line, (128, images)).T

    def mass_of_rows(it):
        def body(j, carry):
            at = pl.ds(pl.multiple_of(j * 128, 128), 128)
            product = share[core, :, at] * rowb[0] + share[2, :, at] * rowb[1]
            mass_out[it, pl.ds(j, 1)] = jnp.sum(product, axis=0, keepdims=True)
            return carry

        lax.fori_loop(0, lanes, body, 0, unroll=2)

    def student_rows():
        loads[3].wait()

        def body(c, carry):
            first, second = carry
            at = pl.ds(pl.multiple_of(c * images, images), images)
            values = sf_ref[at, :].astype(F32)
            sraw[c] = values
            unit = (values * inverse_norm(jnp.sum(values * values, axis=1, keepdims=True))).astype(BF16)
            sbf[at, :] = unit
            wide = unit.astype(F32)
            st[:, at] = wide.T.astype(BF16)
            first = first + jnp.where(c == 0, 0.0, 1.0) * wide
            second = second + jnp.where(c == 1, 0.0, 1.0) * wide
            return first, second

        zero = jnp.zeros((images, depth), F32)
        sums = lax.fori_loop(0, crops, body, (zero, zero))
        for i, values in enumerate(sums):
            high = values.astype(BF16)
            mix[i * images : (i + 1) * images, :] = high
            mix[trows + i * images : trows + (i + 1) * images, :] = (values - high.astype(F32)).astype(BF16)
        racc[...] = jnp.zeros_like(racc)

    def student_prototypes():
        loads[4].wait()

        def body(j, carry):
            at = pl.ds(pl.multiple_of(j * PART, PART), PART)
            values = sp_ref[:, at].astype(F32)
            inverse = inverse_norm(jnp.sum(values * values, axis=0, keepdims=True))
            pscale[:, at] = inverse
            pbf[:, at] = (values * inverse).astype(BF16)
            return carry

        lax.fori_loop(0, columns // PART, body, 0)

    def student_steps(low, high):
        def body(j, carry):
            at = pl.ds(pl.multiple_of(j * WIDTH, WIDTH), WIDTH)
            block = pbf[:, at]
            e = jnp.exp2(
                jnp.dot(sbf[...], block, preferred_element_type=F32) * (math.log2(math.e) / STUDENT_TEMP)
            )
            expo[:, at] = e
            acc = racc[...]
            for lane in range(0, WIDTH, 128):
                acc = acc + e[:, lane : lane + 128]
            racc[...] = acc
            both = jnp.dot(mix[...], block, preferred_element_type=F32)
            mixed[:, at] = (both[:trows] + both[trows:]) * (1.0 / STUDENT_TEMP)
            return carry

        lax.fori_loop(low, high, body, 0)

    def send_exponentials():
        for c in range(crops):
            exp_out[c] = jnp.sum(racc[c * images : (c + 1) * images, :].T, axis=0, keepdims=True)
        send([{"proto": q} for q in proto_peers], exp_out, exp_in.at[p], ex_send.at[6], ex_recv.at[6])

    def student_scales():
        await_all(exp_in, np_, ex_recv.at[6])
        exp_in[pl.ds(p, 1)] = exp_out[...][None]
        for c in range(crops):
            total = jnp.sum(exp_in[:, c], axis=0)
            pairs = 1.0 if c < 2 else 2.0
            scale[c * images : (c + 1) * images, :] = jnp.broadcast_to(
                (pairs * factor) / total, (128, images)
            ).T

        def body(j, carry):
            at = pl.ds(pl.multiple_of(j * 128, 128), 128)
            expo[:, at] = expo[:, at] * scale[...]
            return carry

        lax.fori_loop(0, columns // 128, body, 0)

    send_mass(0)
    loads[2].wait()
    lax.fori_loop(0, half // PART, far_half, 0)
    student_rows()
    send_rows(0)
    student_prototypes()
    student_steps(0, steps // 8)
    row_factors(0, 1.0 / teacher_rows, True)
    mass_of_rows(1)
    send_mass(1)
    student_steps(steps // 8, steps // 2)
    send_rows(1)
    student_steps(steps // 2, steps)
    row_factors(1, 1.0 / teacher_rows, True)
    mass_of_rows(2)
    send_mass(2)
    send_exponentials()
    loss_cols[...] = jnp.zeros_like(loss_cols)
    send_rows(2)
    column_copy = pltpu.make_async_remote_copy(
        col.at[2, core],
        col.at[2, core],
        ex_send.at[10],
        ex_recv.at[10],
        device_id={"batch": z * CORES + other},
        device_id_type=MESH,
    )
    column_copy.start()
    student_scales()
    column_copy.wait_recv()

    def weigh(j, carry):
        at = pl.ds(pl.multiple_of(j * 128, 128), 128)
        for h in range(CORES):
            share[h, :, at] = share[h, :, at] * col[2, h, pl.ds(j, 1)]
        return carry

    lax.fori_loop(0, lanes, weigh, 0)
    row_factors(2, factor, False)

    def core_copy(t):
        return pltpu.make_async_remote_copy(
            wt.at[t, :, other],
            wt_core.at[t],
            core_send.at[t],
            core_recv.at[t],
            device_id={"batch": z * CORES + other},
            device_id_type=MESH,
        )

    def way_of(t, side):
        way = 1 - 2 * lax.rem(t, 2)
        return -way if side else way

    def ring_copy(t, side, s):
        way = way_of(t, side)
        segment = lax.rem(z + way * (hops[side] - s) + nz, nz)
        return pltpu.make_async_remote_copy(
            wt.at[t, segment, core],
            wt_ring.at[t, side, s],
            ring_send.at[t, side, s],
            ring_recv.at[t, side, s],
            device_id={"batch": lax.rem(z + way + nz, nz) * CORES + core},
            device_id_type=MESH,
        )

    def serve(t, phase):
        if phase == 0:
            core_copy(t).wait_recv()
            for segment in range(nz):
                wt[t, segment, pl.ds(core, 1)] += wt_core[t, pl.ds(segment, 1)]
            for side in range(2):
                if hops[side]:
                    ring_copy(t, side, 0).start()
            return
        s = phase - 1
        for side in range(2):
            if s < hops[side]:
                segment = lax.rem(z + way_of(t, side) * (hops[side] - 1 - s) + nz, nz)
                ring_copy(t, side, s).wait_recv()
                wt[t, segment, core] += wt_ring[t, side, s]
                if s + 1 < hops[side]:
                    ring_copy(t, side, s + 1).start()
        if s + 1 == hops[0]:
            at = pl.ds(pl.multiple_of(t * WIDTH, WIDTH), WIDTH)
            gp_ref[:, at] = pscale[:, at] * wt[t, z, core]

    def serve_all(k):
        for phase in range(hops[0], -1, -1):
            t = k - FIRST - LAG * phase

            @pl.when(jnp.logical_and(t >= 0, t < steps))
            def _():
                serve(t, phase)

    def gradient_step(j, carry):
        at = pl.ds(pl.multiple_of(j * WIDTH, WIDTH), WIDTH)
        which = lax.div(j, steps // CORES)
        inside = pl.ds(pl.multiple_of((j - which * (steps // CORES)) * WIDTH, WIDTH), WIDTH)
        row0 = jnp.concatenate([rowb[0, :images, :]] * (WIDTH // 128), axis=1)
        row1 = jnp.concatenate([rowb[0, images:, :]] * (WIDTH // 128), axis=1)
        first = share[which, :images, inside] * row0
        second = share[which, images:, inside] * row1
        loss_cols[...] += jnp.sum(
            first * mixed[:images, at] + second * mixed[images:, at], axis=0, keepdims=True
        )
        both = first + second
        for c in range(crops):
            own_rows = slice(c * images, (c + 1) * images)
            target = second if c == 0 else first if c == 1 else both
            grad[own_rows, at] = (expo[own_rows, at] - target).astype(BF16)
        product = jnp.dot(st[...], grad[:, at], preferred_element_type=F32)
        unit = sp_ref[:, at].astype(F32) * pscale[:, at]
        curvature = jnp.sum(pbf[:, at].astype(F32) * product, axis=0, keepdims=True)
        wt[j] = (product - unit * curvature).reshape(wt.shape[1:])
        core_copy(j).start()
        serve_all(j)
        return carry

    lax.fori_loop(0, steps, gradient_step, 0)

    size = crops // GROUPS

    def send_cot(i):
        group = lax.div(i, np_ - 1)
        q = lax.rem(p + 1 + lax.rem(i, np_ - 1), np_)
        pltpu.make_async_remote_copy(
            cot.at[
                pl.ds(group * size, size), pl.ds(pl.multiple_of(q * own, own), own)
            ],
            cot_in.at[group, p],
            cot_send.at[group],
            cot_recv.at[group],
            device_id={"proto": q},
            device_id_type=MESH,
        ).start()

    def send_more(k):
        rest = max(np_ - 1 - BURST, 0)
        for u in range(EACH):
            n = (k - steps - GROUPS) * EACH + u

            @pl.when(n < GROUPS * rest)
            def _():
                send_cot(lax.div(n, rest) * (np_ - 1) + BURST + lax.rem(n, rest))

    for group in range(GROUPS):
        low = group * size
        cot[low : low + size] = lax.dot_general(
            grad[low * images : (low + size) * images, :],
            pbf[...],
            (((1,), (1,)), ((), ())),
            preferred_element_type=F32,
        ).reshape(size, images, depth)
        for k in range(min(BURST, np_ - 1)):
            send_cot(group * (np_ - 1) + k)
        serve_all(steps + group)

    inverse = row_inv[...]
    portion = row_in[2, pl.ds(p, 1)] + row_in[2, pl.ds(np_ + p, 1)]
    row_inv[...] = portion[0] * inverse
    logs = [jnp.log(jnp.sum(exp_in[:, c], axis=0)) for c in range(crops)]
    shared = functools.reduce(lambda x, y: x + y, logs[2:])
    lossv = row_inv[pl.ds(core * WIDE, 1)] * (logs[1] + shared)
    lossv = lossv + row_inv[pl.ds(core * WIDE + 1, 1)] * (logs[0] + shared)
    for lane in range(0, WIDTH, 128):
        lossv = lossv - loss_cols[:, lane : lane + 128] * (1.0 / factor)
    loss_out[0] = lossv
    send(plane_peers, loss_out.at[0], loss_plane.at[here], ex_send.at[7], ex_recv.at[7])

    def tail(k, carry):
        serve_all(k)
        if np_ - 1 > BURST:
            send_more(k)
        return carry

    middle = steps + GROUPS + LAG
    lax.fori_loop(steps + GROUPS, middle, tail, 0)
    await_all(loss_plane, plane, ex_recv.at[7])
    loss_plane[pl.ds(here, 1)] = loss_out[0][None]
    loss_out[1] = jnp.sum(loss_plane[...], axis=0)
    send(z_peers, loss_out.at[1], loss_z.at[z], ex_send.at[8], ex_recv.at[8])
    lax.fori_loop(middle, steps + LAG * hops[0] + FIRST, tail, 0)

    await_all(loss_z, nz, ex_recv.at[8])
    loss_z[pl.ds(z, 1)] = loss_out[1][None]
    total = jnp.sum(loss_z[...], axis=0)
    loss_ref[...] = jnp.sum(total, axis=1, keepdims=True) * (1.0 / (images_all * PAIRS))

    mine = pl.ds(pl.multiple_of(p * own, own), own)
    for group in range(GROUPS):
        low = group * size
        await_all(cot_in.at[group], np_, cot_recv.at[group])
        cot_in[group, pl.ds(p, 1)] = cot[low : low + size, mine][None]
        total = jnp.sum(cot_in[group], axis=0)
        values = sraw[low : low + size, mine]
        inverse = inverse_norm(jnp.sum(values * values, axis=2, keepdims=True))
        unit = values * inverse
        gf_ref[low : low + size] = inverse * (total - unit * jnp.sum(unit * total, axis=2, keepdims=True))

    for it in range(SK_ITERS):
        await_all(mass_in.at[it], nz, ex_send.at[it])
        await_all(row_in.at[it], plane, ex_send.at[3 + it])
    await_all(exp_in, np_, ex_send.at[6])
    await_all(loss_plane, plane, ex_send.at[7])
    await_all(loss_z, nz, ex_send.at[8])
    teacher_copy.wait_send()
    column_copy.wait_send()
    for group in range(GROUPS):
        await_all(cot_in.at[group], np_, cot_send.at[group])

    def sent(t, carry):
        core_copy(t).wait_send()
        for side in range(2):
            for s in range(hops[side]):
                ring_copy(t, side, s).wait_send()
        return carry

    lax.fori_loop(0, steps, sent, 0)


def hand_on(*refs):
    for source, target in zip(refs[:3], refs[3:]):
        target[...] = source[...]


def on_device(student_features, teacher_features, student_prototypes, teacher_prototypes):
    crops, images, depth = student_features.shape
    columns = student_prototypes.shape[1]
    nb, np_ = lax.axis_size("batch"), lax.axis_size("proto")
    nz = nb // CORES
    rows, trows = crops * images, WIDE * images
    steps, deep, half = columns // WIDTH, depth // nb, columns // CORES
    lanes, own = half // 128, images // np_
    vmem = pltpu.VMEM
    dma = pltpu.SemaphoreType.DMA
    loss, grad_features, grad_prototypes = pl.pallas_call(
        functools.partial(kernel, nb, np_),
        out_shape=(
            jax.ShapeDtypeStruct((1, 1), F32),
            jax.ShapeDtypeStruct((crops, own, depth), F32),
            jax.ShapeDtypeStruct((deep, columns), F32),
        ),
        in_specs=[pl.BlockSpec(memory_space=pl.ANY)] * 4,
        out_specs=[pl.BlockSpec(memory_space=vmem)] * 3,
        scratch_shapes=[
            vmem((rows, depth), BF16),
            vmem((trows, depth), BF16),
            vmem((depth, columns), BF16),
            vmem((depth, columns), BF16),
            vmem((2, trows, depth), BF16),
            vmem((trows, depth), F32),
            vmem((trows, depth), F32),
            vmem((3, trows, half), F32),
            vmem((rows, columns), F32),
            vmem((trows, columns), F32),
            vmem((crops, images, depth), F32),
            vmem((rows, depth), BF16),
            vmem((depth, rows), BF16),
            vmem((2 * trows, depth), BF16),
            vmem((1, columns), F32),
            vmem((rows, 128), F32),
            vmem((rows, 128), F32),
            vmem((rows, columns), BF16),
            vmem((crops, images, depth), F32),
            vmem((GROUPS, np_, crops // GROUPS, own, depth), F32),
            vmem((steps, nz, CORES, deep, WIDTH), F32),
            vmem((steps, nz, deep, WIDTH), F32),
            vmem((steps, 2, nz // 2, deep, WIDTH), F32),
            vmem((2, trows, 128), F32),
            vmem((SK_ITERS, lanes, 128), F32),
            vmem((SK_ITERS, nz, lanes, 128), F32),
            vmem((SK_ITERS, CORES, lanes, 128), F32),
            vmem((SK_ITERS, CORES * WIDE, 128), F32),
            vmem((SK_ITERS, CORES * np_, CORES * WIDE, 128), F32),
            vmem((CORES * WIDE, 128), F32),
            vmem((crops, 1, images), F32),
            vmem((np_, crops, 1, images), F32),
            vmem((1, WIDTH), F32),
            vmem((2, 1, 128), F32),
            vmem((CORES * np_, 1, 128), F32),
            vmem((nz, 1, 128), F32),
            dma((5,)),
            dma((11,)),
            dma((11,)),
            dma((GROUPS,)),
            dma((GROUPS,)),
            dma((steps,)),
            dma((steps,)),
            dma((steps, 2, nz // 2)),
            dma((steps, 2, nz // 2)),
        ],
        compiler_params=pltpu.CompilerParams(
            collective_id=0, has_side_effects=True, vmem_limit_bytes=63 * 1024 * 1024
        ),
    )(
        student_features.reshape(rows, depth),
        teacher_features.reshape(trows, depth),
        student_prototypes,
        teacher_prototypes,
    )
    loss, grad_features, grad_prototypes = pl.pallas_call(
        hand_on,
        out_shape=[jax.ShapeDtypeStruct(r.shape, r.dtype) for r in (loss, grad_features, grad_prototypes)],
        in_specs=[pl.BlockSpec(memory_space=vmem)] * 3,
        out_specs=[pl.BlockSpec(memory_space=vmem)] * 3,
    )(loss, grad_features, grad_prototypes)
    return loss[0, 0], grad_features, grad_prototypes


def solution(mesh):
    return jax.shard_map(
        on_device,
        mesh=mesh,
        in_specs=(P(None, "batch", None), P(None, "batch", None), P(None, "proto"), P(None, "proto")),
        out_specs=(P(), P(None, ("batch", "proto"), None), P("batch", "proto")),
        check_vma=False,
    )
```

```python
import functools
import math

import jax
import jax.numpy as jnp
from jax import lax
from jax.experimental import pallas as pl
from jax.experimental.pallas import tpu as pltpu
from jax.sharding import PartitionSpec as P

WIDE = 2
SK_ITERS = 3
PAIRS = 18
CORES = 2
STUDENT_TEMP = 0.1
TEACHER_TEMP = 0.07
NORM_EPS = 1e-06
MESH = pl.DeviceIdType.MESH
F32 = jnp.float32
BF16 = jnp.bfloat16
WIDTH = 512
PART = 256
FIRST = 2
LAG = 3
GROUPS = 2
BURST = 3
EACH = 5


def inverse_norm(squares):
    return lax.rsqrt(squares + NORM_EPS)


def kernel(
    nb,
    np_,
    sf_hbm,
    tf_hbm,
    sp_hbm,
    tp_hbm,
    loss_ref,
    gf_ref,
    gp_ref,
    sf_ref,
    tf_ref,
    sp_ref,
    pbf,
    tbf,
    tsend,
    trecv,
    share,
    expo,
    mixed,
    sraw,
    sbf,
    st,
    mix,
    pscale,
    racc,
    scale,
    grad,
    cot,
    cot_in,
    wt,
    wt_core,
    wt_ring,
    rowb,
    mass_out,
    mass_in,
    col,
    row_out,
    row_in,
    row_inv,
    exp_out,
    exp_in,
    loss_cols,
    loss_out,
    loss_plane,
    loss_z,
    load_sem,
    ex_send,
    ex_recv,
    cot_send,
    cot_recv,
    core_send,
    core_recv,
    ring_send,
    ring_recv,
):
    b = lax.axis_index("batch")
    p = lax.axis_index("proto")
    nz = nb // CORES
    z, core = lax.div(b, CORES), lax.rem(b, CORES)
    other = 1 - core
    half = share.shape[2]
    lanes = half // 128
    columns = CORES * half
    crops, images, depth = sraw.shape
    steps = columns // WIDTH
    own = images // np_
    images_all = images * nb
    teacher_rows = WIDE * images_all
    clusters = columns * np_
    factor = 1.0 / (images_all * PAIRS * STUDENT_TEMP)
    trows = WIDE * images
    plane = CORES * np_
    here = core * np_ + p
    hops = (nz // 2, nz - 1 - nz // 2)

    far = sorted(range(1, nz), key=lambda k: -min(k, nz - k))
    z_peers = [{"batch": lax.rem(z + k, nz) * CORES + core} for k in far]
    side = math.isqrt(np_)
    y, x = lax.div(p, side), lax.rem(p, side)
    offsets = [(dy, dx) for dy in range(np_ // side) for dx in range(side)][1:]
    offsets.sort(key=lambda o: -min(o[0], np_ // side - o[0]) - min(o[1], side - o[1]))
    proto_peers = [lax.rem(y + dy, np_ // side) * side + lax.rem(x + dx, side) for dy, dx in offsets]
    plane_peers = []
    for q in proto_peers:
        plane_peers += [{"batch": z * CORES + other, "proto": q}, {"proto": q}]
    plane_peers += [{"batch": z * CORES + other}]

    def send(peers, source, target, sends, receives):
        for peer in peers:
            pltpu.make_async_remote_copy(
                source, target, sends, receives, device_id=peer, device_id_type=MESH
            ).start()

    def await_all(block, n, sem):
        view = block.at[pl.ds(0, n - 1)]
        pltpu.make_async_copy(view, view, sem).wait()

    def half_of(ref, which):
        return ref.at[:, pl.ds(pl.multiple_of(which * half, half), half)]

    loads = [
        pltpu.make_async_copy(tf_hbm, tf_ref, load_sem.at[0]),
        pltpu.make_async_copy(half_of(tp_hbm, core), half_of(pbf, core), load_sem.at[1]),
        pltpu.make_async_copy(half_of(tp_hbm, other), half_of(pbf, other), load_sem.at[2]),
        pltpu.make_async_copy(sf_hbm, sf_ref, load_sem.at[3]),
        pltpu.make_async_copy(sp_hbm, sp_ref, load_sem.at[4]),
    ]
    barrier = pltpu.get_barrier_semaphore()
    for load in loads:
        load.start()
    for peer in z_peers + plane_peers:
        pl.semaphore_signal(barrier, inc=1, device_id=peer, device_id_type=MESH)

    loads[0].wait()
    values = tf_ref[...].astype(F32)
    unit = (values * inverse_norm(jnp.sum(values * values, axis=1, keepdims=True))).astype(BF16)
    tbf[0] = unit
    tsend[...] = unit.astype(F32)

    def teacher_unit(which, j):
        at = pl.ds(pl.multiple_of(which * half + j * PART, PART), PART)
        values = pbf[:, at].astype(F32)
        return at, (values * inverse_norm(jnp.sum(values * values, axis=0, keepdims=True))).astype(BF16)

    def teacher_exp(rows, unit):
        logits = jnp.dot(tbf[rows], unit, preferred_element_type=F32)
        return jnp.exp2(logits * (math.log2(math.e) / TEACHER_TEMP))

    def own_half(j, carry):
        at, unit = teacher_unit(core, j)
        pbf[:, at] = unit
        share[core, :, pl.ds(pl.multiple_of(j * PART, PART), PART)] = teacher_exp(0, unit)
        return carry

    def far_half(j, carry):
        at, unit = teacher_unit(other, j)
        share[other, :, pl.ds(pl.multiple_of(j * PART, PART), PART)] = teacher_exp(0, unit)
        return carry

    def other_rows(j, carry):
        at = pl.ds(pl.multiple_of(j * PART, PART), PART)
        e = teacher_exp(1, pbf[:, pl.ds(pl.multiple_of(core * half + j * PART, PART), PART)])
        share[2, :, at] = e
        mass = jnp.sum(share[core, :, at], axis=0, keepdims=True) + jnp.sum(e, axis=0, keepdims=True)
        for lane in range(PART // 128):
            mass_out[0, pl.ds(j * (PART // 128) + lane, 1)] = mass[:, lane * 128 : (lane + 1) * 128]
        return carry

    pl.semaphore_wait(barrier, nz - 1 + plane - 1)
    teacher_copy = pltpu.make_async_remote_copy(
        tsend,
        trecv,
        ex_send.at[9],
        ex_recv.at[9],
        device_id={"batch": z * CORES + other},
        device_id_type=MESH,
    )
    teacher_copy.start()
    loads[1].wait()
    lax.fori_loop(0, half // PART, own_half, 0)
    teacher_copy.wait_recv()
    tbf[1] = trecv[...].astype(BF16)
    lax.fori_loop(0, half // PART, other_rows, 0)

    def send_mass(it):
        send(z_peers, mass_out.at[it], mass_in.at[it, z], ex_send.at[it], ex_recv.at[it])

    def send_rows(it):
        await_all(mass_in.at[it], nz, ex_recv.at[it])
        mass_in[it, pl.ds(z, 1)] = mass_out[it][None]
        col[it, core] = 1.0 / (clusters * jnp.sum(mass_in[it], axis=0))
        for which, block in ((core, core), (2, other)):

            def body(j, acc):
                at = pl.ds(pl.multiple_of(j * 128, 128), 128)
                return acc + share[which, :, at] * col[it, core, pl.ds(j, 1)]

            acc = lax.fori_loop(0, lanes, body, jnp.zeros((trows, 128), F32), unroll=4)
            for crop in range(WIDE):
                row_out[it, pl.ds(block * WIDE + crop, 1)] = jnp.sum(
                    acc[crop * images : (crop + 1) * images].T, axis=0, keepdims=True
                )
        send(plane_peers, row_out.at[it], row_in.at[it, here], ex_send.at[3 + it], ex_recv.at[3 + it])

    def row_factors(it, numerator, both):
        await_all(row_in.at[it], plane, ex_recv.at[3 + it])
        row_in[it, pl.ds(here, 1)] = row_out[it][None]
        row_inv[...] = 1.0 / jnp.sum(row_in[it], axis=0)
        for side, block in ((0, core), (1, other))[: 2 if both else 1]:
            for crop in range(WIDE):
                line = row_inv[pl.ds(block * WIDE + crop, 1)] * numerator
                rowb[side, crop * images : (crop + 1) * images] = jnp.broadcast_to(line, (128, images)).T

    def mass_of_rows(it):
        def body(j, carry):
            at = pl.ds(pl.multiple_of(j * 128, 128), 128)
            product = share[core, :, at] * rowb[0] + share[2, :, at] * rowb[1]
            mass_out[it, pl.ds(j, 1)] = jnp.sum(product, axis=0, keepdims=True)
            return carry

        lax.fori_loop(0, lanes, body, 0, unroll=2)

    def student_rows():
        loads[3].wait()

        def body(c, carry):
            first, second = carry
            at = pl.ds(pl.multiple_of(c * images, images), images)
            values = sf_ref[at, :].astype(F32)
            sraw[c] = values
            unit = (values * inverse_norm(jnp.sum(values * values, axis=1, keepdims=True))).astype(BF16)
            sbf[at, :] = unit
            wide = unit.astype(F32)
            st[:, at] = wide.T.astype(BF16)
            first = first + jnp.where(c == 0, 0.0, 1.0) * wide
            second = second + jnp.where(c == 1, 0.0, 1.0) * wide
            return first, second

        zero = jnp.zeros((images, depth), F32)
        sums = lax.fori_loop(0, crops, body, (zero, zero))
        for i, values in enumerate(sums):
            high = values.astype(BF16)
            mix[i * images : (i + 1) * images, :] = high
            mix[trows + i * images : trows + (i + 1) * images, :] = (values - high.astype(F32)).astype(BF16)
        racc[...] = jnp.zeros_like(racc)

    def student_prototypes():
        loads[4].wait()

        def body(j, carry):
            at = pl.ds(pl.multiple_of(j * PART, PART), PART)
            values = sp_ref[:, at].astype(F32)
            inverse = inverse_norm(jnp.sum(values * values, axis=0, keepdims=True))
            pscale[:, at] = inverse
            pbf[:, at] = (values * inverse).astype(BF16)
            return carry

        lax.fori_loop(0, columns // PART, body, 0)

    def student_steps(low, high):
        def body(j, carry):
            at = pl.ds(pl.multiple_of(j * WIDTH, WIDTH), WIDTH)
            block = pbf[:, at]
            e = jnp.exp2(
                jnp.dot(sbf[...], block, preferred_element_type=F32) * (math.log2(math.e) / STUDENT_TEMP)
            )
            expo[:, at] = e
            acc = racc[...]
            for lane in range(0, WIDTH, 128):
                acc = acc + e[:, lane : lane + 128]
            racc[...] = acc
            both = jnp.dot(mix[...], block, preferred_element_type=F32)
            mixed[:, at] = (both[:trows] + both[trows:]) * (1.0 / STUDENT_TEMP)
            return carry

        lax.fori_loop(low, high, body, 0)

    def send_exponentials():
        for c in range(crops):
            exp_out[c] = jnp.sum(racc[c * images : (c + 1) * images, :].T, axis=0, keepdims=True)
        send([{"proto": q} for q in proto_peers], exp_out, exp_in.at[p], ex_send.at[6], ex_recv.at[6])

    def student_scales():
        await_all(exp_in, np_, ex_recv.at[6])
        exp_in[pl.ds(p, 1)] = exp_out[...][None]
        for c in range(crops):
            total = jnp.sum(exp_in[:, c], axis=0)
            pairs = 1.0 if c < 2 else 2.0
            scale[c * images : (c + 1) * images, :] = jnp.broadcast_to(
                (pairs * factor) / total, (128, images)
            ).T

        def body(j, carry):
            at = pl.ds(pl.multiple_of(j * 128, 128), 128)
            expo[:, at] = expo[:, at] * scale[...]
            return carry

        lax.fori_loop(0, columns // 128, body, 0)

    send_mass(0)
    loads[2].wait()
    lax.fori_loop(0, half // PART, far_half, 0)
    student_rows()
    send_rows(0)
    student_prototypes()
    student_steps(0, steps // 8)
    row_factors(0, 1.0 / teacher_rows, True)
    mass_of_rows(1)
    send_mass(1)
    student_steps(steps // 8, steps // 2)
    send_rows(1)
    student_steps(steps // 2, steps)
    row_factors(1, 1.0 / teacher_rows, True)
    mass_of_rows(2)
    send_mass(2)
    send_exponentials()
    loss_cols[...] = jnp.zeros_like(loss_cols)
    send_rows(2)
    column_copy = pltpu.make_async_remote_copy(
        col.at[2, core],
        col.at[2, core],
        ex_send.at[10],
        ex_recv.at[10],
        device_id={"batch": z * CORES + other},
        device_id_type=MESH,
    )
    column_copy.start()
    student_scales()
    column_copy.wait_recv()

    def weigh(j, carry):
        at = pl.ds(pl.multiple_of(j * 128, 128), 128)
        for h in range(CORES):
            share[h, :, at] = share[h, :, at] * col[2, h, pl.ds(j, 1)]
        return carry

    lax.fori_loop(0, lanes, weigh, 0)
    row_factors(2, factor, False)

    def core_copy(t):
        return pltpu.make_async_remote_copy(
            wt.at[t, :, other],
            wt_core.at[t],
            core_send.at[t],
            core_recv.at[t],
            device_id={"batch": z * CORES + other},
            device_id_type=MESH,
        )

    def way_of(t, side):
        way = 1 - 2 * lax.rem(t, 2)
        return -way if side else way

    def ring_copy(t, side, s):
        way = way_of(t, side)
        segment = lax.rem(z + way * (hops[side] - s) + nz, nz)
        return pltpu.make_async_remote_copy(
            wt.at[t, segment, core],
            wt_ring.at[t, side, s],
            ring_send.at[t, side, s],
            ring_recv.at[t, side, s],
            device_id={"batch": lax.rem(z + way + nz, nz) * CORES + core},
            device_id_type=MESH,
        )

    def serve(t, phase):
        if phase == 0:
            core_copy(t).wait_recv()
            for segment in range(nz):
                wt[t, segment, pl.ds(core, 1)] += wt_core[t, pl.ds(segment, 1)]
            for side in range(2):
                if hops[side]:
                    ring_copy(t, side, 0).start()
            core_copy(t).wait_send()
            return
        s = phase - 1
        for side in range(2):
            if s < hops[side]:
                segment = lax.rem(z + way_of(t, side) * (hops[side] - 1 - s) + nz, nz)
                ring_copy(t, side, s).wait_recv()
                wt[t, segment, core] += wt_ring[t, side, s]
                if s + 1 < hops[side]:
                    ring_copy(t, side, s + 1).start()
                ring_copy(t, side, s).wait_send()
        if s + 1 == hops[0]:
            at = pl.ds(pl.multiple_of(t * WIDTH, WIDTH), WIDTH)
            gp_ref[:, at] = pscale[:, at] * wt[t, z, core]

    def serve_all(k):
        for phase in range(hops[0], -1, -1):
            t = k - FIRST - LAG * phase

            @pl.when(jnp.logical_and(t >= 0, t < steps))
            def _():
                serve(t, phase)

    def gradient_step(j, carry):
        at = pl.ds(pl.multiple_of(j * WIDTH, WIDTH), WIDTH)
        which = lax.div(j, steps // CORES)
        inside = pl.ds(pl.multiple_of((j - which * (steps // CORES)) * WIDTH, WIDTH), WIDTH)
        row0 = jnp.concatenate([rowb[0, :images, :]] * (WIDTH // 128), axis=1)
        row1 = jnp.concatenate([rowb[0, images:, :]] * (WIDTH // 128), axis=1)
        first = share[which, :images, inside] * row0
        second = share[which, images:, inside] * row1
        loss_cols[...] += jnp.sum(
            first * mixed[:images, at] + second * mixed[images:, at], axis=0, keepdims=True
        )
        both = first + second
        for c in range(crops):
            own_rows = slice(c * images, (c + 1) * images)
            target = second if c == 0 else first if c == 1 else both
            grad[own_rows, at] = (expo[own_rows, at] - target).astype(BF16)
        product = jnp.dot(st[...], grad[:, at], preferred_element_type=F32)
        unit = sp_ref[:, at].astype(F32) * pscale[:, at]
        curvature = jnp.sum(pbf[:, at].astype(F32) * product, axis=0, keepdims=True)
        wt[j] = (product - unit * curvature).reshape(wt.shape[1:])
        core_copy(j).start()
        serve_all(j)
        return carry

    lax.fori_loop(0, steps, gradient_step, 0)

    size = crops // GROUPS

    def send_cot(i):
        group = lax.div(i, np_ - 1)
        q = lax.rem(p + 1 + lax.rem(i, np_ - 1), np_)
        pltpu.make_async_remote_copy(
            cot.at[
                pl.ds(group * size, size), pl.ds(pl.multiple_of(q * own, own), own)
            ],
            cot_in.at[group, p],
            cot_send.at[group],
            cot_recv.at[group],
            device_id={"proto": q},
            device_id_type=MESH,
        ).start()

    def send_more(k):
        rest = max(np_ - 1 - BURST, 0)
        for u in range(EACH):
            n = (k - steps - GROUPS) * EACH + u

            @pl.when(n < GROUPS * rest)
            def _():
                send_cot(lax.div(n, rest) * (np_ - 1) + BURST + lax.rem(n, rest))

    for group in range(GROUPS):
        low = group * size
        cot[low : low + size] = lax.dot_general(
            grad[low * images : (low + size) * images, :],
            pbf[...],
            (((1,), (1,)), ((), ())),
            preferred_element_type=F32,
        ).reshape(size, images, depth)
        for k in range(min(BURST, np_ - 1)):
            send_cot(group * (np_ - 1) + k)
        serve_all(steps + group)

    for it in range(SK_ITERS):
        await_all(mass_in.at[it], nz, ex_send.at[it])
        await_all(row_in.at[it], plane, ex_send.at[3 + it])
    await_all(exp_in, np_, ex_send.at[6])
    teacher_copy.wait_send()
    column_copy.wait_send()

    inverse = row_inv[...]
    portion = row_in[2, pl.ds(p, 1)] + row_in[2, pl.ds(np_ + p, 1)]
    row_inv[...] = portion[0] * inverse
    logs = [jnp.log(jnp.sum(exp_in[:, c], axis=0)) for c in range(crops)]
    shared = functools.reduce(lambda x, y: x + y, logs[2:])
    lossv = row_inv[pl.ds(core * WIDE, 1)] * (logs[1] + shared)
    lossv = lossv + row_inv[pl.ds(core * WIDE + 1, 1)] * (logs[0] + shared)
    for lane in range(0, WIDTH, 128):
        lossv = lossv - loss_cols[:, lane : lane + 128] * (1.0 / factor)
    loss_out[0] = lossv
    send(plane_peers, loss_out.at[0], loss_plane.at[here], ex_send.at[7], ex_recv.at[7])

    def tail(k, carry):
        serve_all(k)
        if np_ - 1 > BURST:
            send_more(k)
        return carry

    middle = steps + GROUPS + LAG
    lax.fori_loop(steps + GROUPS, middle, tail, 0)
    await_all(loss_plane, plane, ex_recv.at[7])
    loss_plane[pl.ds(here, 1)] = loss_out[0][None]
    loss_out[1] = jnp.sum(loss_plane[...], axis=0)
    send(z_peers, loss_out.at[1], loss_z.at[z], ex_send.at[8], ex_recv.at[8])
    lax.fori_loop(middle, steps + LAG * hops[0] + FIRST, tail, 0)

    await_all(loss_z, nz, ex_recv.at[8])
    loss_z[pl.ds(z, 1)] = loss_out[1][None]
    total = jnp.sum(loss_z[...], axis=0)
    loss_ref[...] = jnp.sum(total, axis=1, keepdims=True) * (1.0 / (images_all * PAIRS))

    mine = pl.ds(pl.multiple_of(p * own, own), own)
    for group in range(GROUPS):
        low = group * size
        await_all(cot_in.at[group], np_, cot_recv.at[group])
        cot_in[group, pl.ds(p, 1)] = cot[low : low + size, mine][None]
        total = jnp.sum(cot_in[group], axis=0)
        values = sraw[low : low + size, mine]
        inverse = inverse_norm(jnp.sum(values * values, axis=2, keepdims=True))
        unit = values * inverse
        gf_ref[low : low + size] = inverse * (total - unit * jnp.sum(unit * total, axis=2, keepdims=True))

    await_all(loss_plane, plane, ex_send.at[7])
    await_all(loss_z, nz, ex_send.at[8])
    for group in range(GROUPS):
        await_all(cot_in.at[group], np_, cot_send.at[group])


def hand_on(*refs):
    for source, target in zip(refs[:3], refs[3:]):
        target[...] = source[...]


def on_device(student_features, teacher_features, student_prototypes, teacher_prototypes):
    crops, images, depth = student_features.shape
    columns = student_prototypes.shape[1]
    nb, np_ = lax.axis_size("batch"), lax.axis_size("proto")
    nz = nb // CORES
    rows, trows = crops * images, WIDE * images
    steps, deep, half = columns // WIDTH, depth // nb, columns // CORES
    lanes, own = half // 128, images // np_
    vmem = pltpu.VMEM
    dma = pltpu.SemaphoreType.DMA
    loss, grad_features, grad_prototypes = pl.pallas_call(
        functools.partial(kernel, nb, np_),
        out_shape=(
            jax.ShapeDtypeStruct((1, 1), F32),
            jax.ShapeDtypeStruct((crops, own, depth), F32),
            jax.ShapeDtypeStruct((deep, columns), F32),
        ),
        in_specs=[pl.BlockSpec(memory_space=pl.ANY)] * 4,
        out_specs=[pl.BlockSpec(memory_space=vmem)] * 3,
        scratch_shapes=[
            vmem((rows, depth), BF16),
            vmem((trows, depth), BF16),
            vmem((depth, columns), BF16),
            vmem((depth, columns), BF16),
            vmem((2, trows, depth), BF16),
            vmem((trows, depth), F32),
            vmem((trows, depth), F32),
            vmem((3, trows, half), F32),
            vmem((rows, columns), F32),
            vmem((trows, columns), F32),
            vmem((crops, images, depth), F32),
            vmem((rows, depth), BF16),
            vmem((depth, rows), BF16),
            vmem((2 * trows, depth), BF16),
            vmem((1, columns), F32),
            vmem((rows, 128), F32),
            vmem((rows, 128), F32),
            vmem((rows, columns), BF16),
            vmem((crops, images, depth), F32),
            vmem((GROUPS, np_, crops // GROUPS, own, depth), F32),
            vmem((steps, nz, CORES, deep, WIDTH), F32),
            vmem((steps, nz, deep, WIDTH), F32),
            vmem((steps, 2, nz // 2, deep, WIDTH), F32),
            vmem((2, trows, 128), F32),
            vmem((SK_ITERS, lanes, 128), F32),
            vmem((SK_ITERS, nz, lanes, 128), F32),
            vmem((SK_ITERS, CORES, lanes, 128), F32),
            vmem((SK_ITERS, CORES * WIDE, 128), F32),
            vmem((SK_ITERS, CORES * np_, CORES * WIDE, 128), F32),
            vmem((CORES * WIDE, 128), F32),
            vmem((crops, 1, images), F32),
            vmem((np_, crops, 1, images), F32),
            vmem((1, WIDTH), F32),
            vmem((2, 1, 128), F32),
            vmem((CORES * np_, 1, 128), F32),
            vmem((nz, 1, 128), F32),
            dma((5,)),
            dma((11,)),
            dma((11,)),
            dma((GROUPS,)),
            dma((GROUPS,)),
            dma((steps,)),
            dma((steps,)),
            dma((steps, 2, nz // 2)),
            dma((steps, 2, nz // 2)),
        ],
        compiler_params=pltpu.CompilerParams(
            collective_id=0, has_side_effects=True, vmem_limit_bytes=63 * 1024 * 1024
        ),
    )(
        student_features.reshape(rows, depth),
        teacher_features.reshape(trows, depth),
        student_prototypes,
        teacher_prototypes,
    )
    loss, grad_features, grad_prototypes = pl.pallas_call(
        hand_on,
        out_shape=[jax.ShapeDtypeStruct(r.shape, r.dtype) for r in (loss, grad_features, grad_prototypes)],
        in_specs=[pl.BlockSpec(memory_space=vmem)] * 3,
        out_specs=[pl.BlockSpec(memory_space=vmem)] * 3,
    )(loss, grad_features, grad_prototypes)
    return loss[0, 0], grad_features, grad_prototypes


def solution(mesh):
    return jax.shard_map(
        on_device,
        mesh=mesh,
        in_specs=(P(None, "batch", None), P(None, "batch", None), P(None, "proto"), P(None, "proto")),
        out_specs=(P(), P(None, ("batch", "proto"), None), P("batch", "proto")),
        check_vma=False,
    )
```
